32 devices in a mesh: group: 2 (over x), leaf: 16 (over z, y, core).
Axes of the slice: x: 2, y: 2, z: 4, core: 2. Of those that a mesh axis runs over, the one named last changes fastest.
Arguments:
- points: bfloat16 [32768, 64], P(('group', 'leaf')), may hold values from -6 to 6
- weights: bfloat16 [32768, 128], P(('group', 'leaf')), may hold values from -6 to 6
- interp: bfloat16 [32768, 256], P(('group', 'leaf')), may hold values from -0.1875 to 0.1875
- cluster_interp: bfloat16 [8192, 512], P(('group', 'leaf')), may hold values from -0.09375 to 0.09375
- skeleton_rows: int32 [32, 256], P(('group', 'leaf')), may hold values from 0 to 1023, as said below
- near_flags: int32 [32, 5], P(('group', 'leaf')), may hold values from 0 to 1, as said below
- cluster_rows: int32 [2, 512], P('group'), may hold values from 0 to 4095, as said below
Outputs:
- potential: bfloat16 [32768, 128], P(('group', 'leaf'))
The draws below stay inside these ranges and needn't reach their ends.
Inputs may be any that keep to these rules, and one draw needn't show every extreme that they name: `skeleton_rows`: within a row the values are distinct. `near_flags`: the middle column is 1; a column is 0 where the leaf it names lies outside the leaf's group. `cluster_rows`: within a row the values are distinct.
All inputs are finite; a program needn't handle non-finite values.
Results may differ from the reference program's by a relative error of at most 0.0063.
Values may be sent and summed in bfloat16 or wider, within the bound.
No kernel may reach another device: no remote copies, remote signals or barrier semaphores. Data moves between devices by JAX's collectives and lax.ppermute only.
A program may use at most 64 MiB of HBM per device.

```python
import jax
import jax.numpy as jnp
from jax import lax

F = 64
R = 128
LEAF = 1024
SK = 256
CSK = 512
REACH = 2
LEAVES = 32
CLUSTERS = 2
NPTS = 32768
N_GROUP = 2
N_LEAF = 16


def draw_skeleton_rows(key, part):
    keys = jax.random.split(jax.random.fold_in(key, 3), LEAVES)
    return jax.vmap(lambda single: jax.random.permutation(single, LEAF)[:SK])(keys).astype(jnp.int32)


def draw_cluster_rows(key, part):
    keys = jax.random.split(jax.random.fold_in(key, 5), CLUSTERS)
    return jax.vmap(lambda single: jax.random.permutation(single, 16 * SK)[:CSK])(keys).astype(jnp.int32)


def draw_near_flags(key, part):
    first_key, second_key = jax.random.split(jax.random.fold_in(key, 11))
    flag_count = 2 * REACH + 1
    levels = jax.random.randint(first_key, (LEAVES, 1), 0, 5)
    rolled = jax.random.randint(second_key, (LEAVES, flag_count), 0, 4)
    offsets = jnp.arange(flag_count, dtype=jnp.int32)[None, :] - REACH
    places = jnp.arange(LEAVES, dtype=jnp.int32)[:, None] % N_LEAF
    inside = (places + offsets >= 0) & (places + offsets < N_LEAF)
    chosen = jnp.where(inside & (rolled < levels), 1, 0)
    return jnp.where(offsets == 0, 1, chosen).astype(jnp.int32)


def steps_of(rng, extent, pieces, low, largest):
    level, own = 1.0, jax.random.fold_in(rng, 6)
    for dim, blocks in pieces:
        heights = jnp.exp(jax.random.uniform(jax.random.fold_in(own, dim), (blocks,), jnp.float32, low / len(pieces), largest / len(pieces)))
        level = level * jnp.repeat(heights, extent[dim] // blocks).reshape([-1 if axis == dim else 1 for axis in range(len(extent))])
    return level


def normal_values(stream_key, shape, spread, bound, pieces=(), kind=jnp.bfloat16):
    values = jax.random.normal(stream_key, shape, jnp.float32) * spread
    if len(pieces) > 0:
        values = steps_of(stream_key, shape, pieces, -0.22, 0.18) * values
    return jnp.clip(values, min=-bound, max=bound).astype(kind)


def setup_inputs(seed: int = 0) -> dict:
    seeds = jax.random.split(jax.random.key(seed), 8)
    points = normal_values(seeds[0], (NPTS, F), 1.0, 6.0, ((0, 32),))
    weights = normal_values(seeds[1], (NPTS, R), 1.0, 6.0, ((0, 32),))
    interp = normal_values(seeds[2], (NPTS, SK), LEAF ** -0.5, 0.1875, ((0, 32),))
    cluster_interp = normal_values(seeds[3], (LEAVES * SK, CSK), (16 * SK) ** -0.5, 0.09375, ((0, 32),))
    skeleton_rows = draw_skeleton_rows(jax.random.fold_in(seeds[7], 71), 0)
    near_flags = draw_near_flags(jax.random.fold_in(seeds[7], 71), 0)
    cluster_rows = draw_cluster_rows(jax.random.fold_in(seeds[7], 71), 0)
    return dict(points=points, weights=weights, interp=interp, cluster_interp=cluster_interp, skeleton_rows=skeleton_rows, near_flags=near_flags, cluster_rows=cluster_rows)


def kernel_tile(targets, sources):
    target_sq_norm_values = jnp.sum(jnp.square(targets.astype(jnp.float32)), axis=1)
    source_norm = jnp.sum(jnp.square(sources.astype(jnp.float32)), axis=1)
    inner_term = lax.dot_general(targets, sources, (((1,), (1,)), ((), ())), preferred_element_type=jnp.float32)
    scaled = (target_sq_norm_values[:, None] + source_norm[None, :] - 2.0 * inner_term) * (2.0 / targets.shape[1])
    return jnp.exp(-scaled).astype(jnp.bfloat16)


def reference(points, weights, interp, cluster_interp, skeleton_rows, near_flags, cluster_rows):
    leaf_nodes = N_GROUP * N_LEAF
    clusters = leaf_nodes // 16
    leaf_points = points.reshape(leaf_nodes, LEAF, F)
    leaf_weight_values = weights.reshape(leaf_nodes, LEAF, R)
    leaf_interpolant = interp.reshape(leaf_nodes, LEAF, SK)
    skeleton = jnp.take_along_axis(leaf_points, skeleton_rows.astype(jnp.int32)[:, :, None], axis=1)
    skeleton_charges = jnp.einsum("cbm,cbx->cmx", leaf_interpolant.astype(jnp.float32), leaf_weight_values.astype(jnp.float32)).astype(jnp.bfloat16)
    cluster_mass = jnp.einsum("cajk,cajr->ckr", cluster_interp.reshape(clusters, 16, SK, CSK).astype(jnp.float32), skeleton_charges.reshape(clusters, 16, SK, R).astype(jnp.float32)).astype(jnp.bfloat16)
    cluster_points = jnp.take_along_axis(skeleton.reshape(clusters, 16 * SK, F), cluster_rows.astype(jnp.int32)[:, :, None], axis=1)
    flattened_points = cluster_points.reshape(clusters * CSK, F)
    flat_mass = cluster_mass.reshape(clusters * CSK, R)
    per_group = (N_LEAF // 16) * CSK
    row_group = jnp.arange(clusters * CSK, dtype=jnp.int32) // per_group
    flag_count = 2 * REACH + 1
    offsets = jnp.arange(flag_count, dtype=jnp.int32) - REACH

    def one_leaf(target):
        group_index = target // N_LEAF
        place = target % N_LEAF
        nearby_row = near_flags[target]
        near_field = jnp.zeros((LEAF, R), jnp.float32)
        for column in range(flag_count):
            source = jnp.clip(target + column - REACH, 0, leaf_nodes - 1).astype(jnp.int32)
            block_kernel = kernel_tile(leaf_points[target], leaf_points[source])
            near_field = near_field + nearby_row[column].astype(jnp.float32) * jnp.dot(block_kernel, leaf_weight_values[source], preferred_element_type=jnp.float32)
        sibling_points = lax.dynamic_slice_in_dim(skeleton, group_index * N_LEAF, N_LEAF, 0).reshape(N_LEAF * SK, F)
        sibling_mass = lax.dynamic_slice_in_dim(skeleton_charges, group_index * N_LEAF, N_LEAF, 0).reshape(N_LEAF * SK, R)
        distance = jnp.arange(N_LEAF * SK, dtype=jnp.int32) // SK - place
        listed = jnp.sum((distance[:, None] == offsets[None, :]).astype(jnp.int32) * nearby_row[None, :], axis=1)
        kept_rows = (1 - listed).astype(jnp.bfloat16)
        sibling = jnp.dot(kernel_tile(skeleton[target], sibling_points), sibling_mass * kept_rows[:, None], preferred_element_type=jnp.float32)
        far_rows = (row_group != group_index).astype(jnp.bfloat16)
        distant = jnp.dot(kernel_tile(skeleton[target], flattened_points), flat_mass * far_rows[:, None], preferred_element_type=jnp.float32)
        coarse_field = (sibling + distant).astype(jnp.bfloat16)
        return (near_field + jnp.dot(leaf_interpolant[target], coarse_field, preferred_element_type=jnp.float32)).astype(jnp.bfloat16)

    result = lax.map(one_leaf, jnp.arange(leaf_nodes, dtype=jnp.int32))
    return result.reshape(leaf_nodes * LEAF, R)
```

```python
import functools
import math

import jax
import jax.numpy as jnp
from jax import lax
from jax.experimental import pallas as pl
from jax.experimental.pallas import tpu as pltpu
from jax.sharding import PartitionSpec as P

BF16 = jnp.bfloat16
F32 = jnp.float32
VMEM_BYTES = 24 * 1024 * 1024
TARGET_ROWS = 256
SOURCE_ROWS = 512


def vmem():
    return pl.BlockSpec(memory_space=pltpu.VMEM)


def smem():
    return pl.BlockSpec(memory_space=pltpu.SMEM)


def call(body, outs, ins, scratch=(), flops=0, moved=0):
    specs, args = [], []
    for item in ins:
        if isinstance(item, tuple):
            specs.append(smem())
            args.append(item[0])
        else:
            specs.append(vmem())
            args.append(item)
    return pl.pallas_call(
        body,
        out_shape=[jax.ShapeDtypeStruct(shape, dtype) for shape, dtype in outs],
        in_specs=specs,
        out_specs=[vmem() for _ in outs],
        scratch_shapes=[pltpu.VMEM(shape, dtype) for shape, dtype in scratch],
        compiler_params=pltpu.CompilerParams(vmem_limit_bytes=VMEM_BYTES),
        cost_estimate=pl.CostEstimate(flops=flops, bytes_accessed=moved, transcendentals=0),
    )(*args)


def dot_nt(a, b):
    return lax.dot_general(a, b, (((1,), (1,)), ((), ())), preferred_element_type=F32)


def dot_tn(a, b):
    return lax.dot_general(a, b, (((0,), (0,)), ((), ())), preferred_element_type=F32)


def dot_nn(a, b):
    return jnp.dot(a, b, preferred_element_type=F32)


def pack_halves(values):
    half = values.shape[0] // 2
    return jnp.concatenate([values[:half], values[half:]], axis=1)


def extended(values, features, as_target):
    lane = lax.broadcasted_iota(jnp.int32, values.shape, 1)
    kept = jnp.where(lane < features, values, 0.0)
    norm = -0.5 * jnp.sum(kept * kept, axis=1, keepdims=True)
    high = norm.astype(BF16).astype(F32)
    rest = norm - high
    middle = rest.astype(BF16).astype(F32)
    low = rest - middle
    first = features if as_target else features + 3
    ones = features + 3 if as_target else features
    out = jnp.where((lane >= ones) & (lane < ones + 3), 1.0, kept)
    out = jnp.where(lane == first, high, out)
    out = jnp.where(lane == first + 1, middle, out)
    out = jnp.where(lane == first + 2, low, out)
    return out.astype(BF16)


def extended_halves(packed, features, as_target):
    wide = packed.astype(F32)
    return (
        extended(wide, features, as_target),
        extended(pltpu.roll(wide, features, 1), features, as_target),
    )


def exponent_scale(features):
    return 4.0 / features * math.log2(math.e)


def kernel_values(targets, sources, features):
    return jnp.exp2(dot_nt(targets, sources) * exponent_scale(features)).astype(BF16)


def product(targets, source_ref, mass_ref, first, rows, features, mass_first=0):
    total = None
    step = min(SOURCE_ROWS, rows)
    for start in range(0, rows, step):
        tile = kernel_values(targets, source_ref[first + start : first + start + step, :], features)
        term = dot_nn(tile, mass_ref[mass_first + start : mass_first + start + step, :])
        total = term if total is None else total + term
    return total


def xor_exchange(value, axis, mask):
    return lax.ppermute(value, axis, [(i, i ^ mask) for i in range(lax.axis_size(axis))])


def pack_kernel(points_ref, weights_ref, halo_ref):
    half = points_ref.shape[0] // 2
    halo_ref[:half, :] = pack_halves(points_ref[...].astype(F32)).astype(BF16)
    halo_ref[half:, :] = weights_ref[...]


def skeleton_kernel(
    points_ref, weights_ref, interp_ref, ci_ref, rows_ref, ids_ref, sv_ref, sum_ref, send_ref, u_ref, c_ref
):
    leaf = lax.axis_index("leaf")
    points, skeleton_count = points_ref.shape[0], interp_ref.shape[1]
    cluster_count, picked = ids_ref.shape
    members = lax.axis_size("leaf") // cluster_count
    core = leaf % 2
    one = (
        lax.broadcasted_iota(jnp.int32, (points, skeleton_count), 0) == rows_ref[...]
    ).astype(F32).astype(BF16)
    skeleton = dot_tn(one, points_ref[...])
    charges = dot_tn(interp_ref[...], weights_ref[...]).astype(BF16)
    half = skeleton_count // 2
    sv_ref[:half, :] = pack_halves(skeleton).astype(BF16)
    sv_ref[half:, :] = charges
    u_ref[...] = dot_tn(ci_ref[...], charges)
    ids = ids_ref[pl.ds(leaf // members, 1), :] - (leaf % members) * skeleton_count
    chosen = (
        lax.broadcasted_iota(jnp.int32, (skeleton_count, picked), 0) == ids
    ).astype(F32).astype(BF16)
    cluster = dot_tn(chosen, skeleton.astype(BF16))
    part = picked // 2
    c_ref[: part // 2, :] = pack_halves(cluster[:part])
    c_ref[part // 2 :, :] = pack_halves(cluster[part:])
    sum_ref[:part, :] = u_ref[pl.ds(core * part, part), :]
    sum_ref[part:, :] = c_ref[pl.ds(core * (part // 2), part // 2), :]
    send_ref[:part, :] = u_ref[pl.ds((1 - core) * part, part), :].astype(BF16)
    send_ref[part:, :] = c_ref[pl.ds((1 - core) * (part // 2), part // 2), :].astype(BF16)


def first_add_kernel(flags_ref, sum_ref, got_ref, sv_ref, new_ref, send_ref):
    rows = sum_ref.shape[0]
    half = send_ref.shape[0] - 16 - rows
    total = sum_ref[...] + got_ref[...].astype(F32)
    new_ref[...] = total
    send_ref[:rows, :] = total.astype(BF16)
    send_ref[rows : rows + half, :] = sv_ref[:half, :]
    lane = lax.broadcasted_iota(jnp.int32, (16, send_ref.shape[1]), 1)
    row = jnp.zeros(lane.shape, F32)
    for column in range(flags_ref.shape[1]):
        row = jnp.where(lane == column, flags_ref[0, column].astype(F32), row)
    send_ref[rows + half :, :] = row.astype(BF16)


def add_kernel(sum_ref, got_ref, new_ref, send_ref):
    rows = sum_ref.shape[0]
    total = sum_ref[...] + got_ref[:rows, :].astype(F32)
    new_ref[...] = total
    send_ref[...] = total.astype(BF16)


def near_tile(targets_ref, halo_ref, source_ref, near_ref, features):
    half = source_ref.shape[0] // 2
    low, high = extended_halves(halo_ref[:half, :], features, False)
    source_ref[:half, :] = low
    source_ref[half:, :] = high
    for start in range(0, targets_ref.shape[0], TARGET_ROWS):
        rows = slice(start, start + TARGET_ROWS)
        near_ref[rows, :] += product(
            targets_ref[rows, :], source_ref, halo_ref, 0, 2 * half, features, half
        )


def near_kernel(stage, features, flags_ref, own_ref, across_ref, *refs):
    leaf = lax.axis_index("leaf")
    core, chip = leaf % 2, (leaf // 2) % 2
    reach = (flags_ref.shape[1] - 1) // 2
    side, beside = 1 - 2 * core, 1 - 2 * chip
    if stage == 0:
        targets_ref, near_ref, source_ref = refs
        half = targets_ref.shape[0] // 2
        low, high = extended_halves(own_ref[:half, :], features, True)
        targets_ref[:half, :] = low
        targets_ref[half:, :] = high
        near_ref[...] = jnp.zeros_like(near_ref)
        distances, here = (0, side), core == core
    else:
        targets_ref, before_ref, near_ref, source_ref = refs
        near_ref[...] = before_ref[...]
        distances = (2 * beside if stage == 1 else -2 * beside, -side)
        here = core != chip if stage == 1 else core == chip

    @pl.when(flags_ref[0, reach + distances[0]] != 0)
    def _():
        near_tile(targets_ref, own_ref, source_ref, near_ref, features)

    @pl.when((flags_ref[0, reach + distances[1]] != 0) & here)
    def _():
        near_tile(targets_ref, across_ref, source_ref, near_ref, features)


def sibling_kernel(masks, reduced, features, flags_ref, got_ref, *refs):
    pieces, refs = refs[: len(masks)], refs[len(masks) :]
    own_ref, send_ref, low_ref, high_ref, mine_ref, other_ref, targets_ref = refs
    leaf = lax.axis_index("leaf")
    columns = flags_ref.shape[1]
    reach = (columns - 1) // 2
    half = pieces[0].shape[0] // 3
    got_rows = got_ref.shape[0]
    other_points = got_ref[got_rows - 16 - half : got_rows - 16, :]
    other_flags = got_ref[got_rows - 16 :, :].astype(F32)[:1, :]
    lane = lax.broadcasted_iota(jnp.int32, other_flags.shape, 1)
    total = len(masks) * half
    for position, (mask, piece) in enumerate(zip(masks, pieces)):
        source = leaf ^ mask
        rows = slice(position * half, (position + 1) * half)
        later = slice(total + position * half, total + (position + 1) * half)
        low, high = extended_halves(piece[:half, :], features, False)
        low_ref[rows, :] = low
        high_ref[rows, :] = high
        mine = source - leaf + reach
        listed = flags_ref[0, jnp.clip(mine, 0, columns - 1)]
        kept = jnp.where((mine >= 0) & (mine < columns), 1 - listed, 1).astype(F32)
        flagged = jnp.where(lane == source - (leaf ^ reduced) + reach, other_flags, 0.0)
        kept_other = 1.0 - jnp.sum(flagged, axis=1, keepdims=True)
        mass = piece[half:, :].astype(F32)
        for ref, factor in ((mine_ref, kept), (other_ref, kept_other)):
            scaled = (mass * factor).astype(BF16)
            ref[rows, :] = scaled[:half]
            ref[later, :] = scaled[half:]
    for start, packed in ((0, pieces[0][:half, :]), (2 * half, other_points)):
        low, high = extended_halves(packed, features, True)
        targets_ref[start : start + half, :] = low
        targets_ref[start + half : start + 2 * half, :] = high
    for start, mass_ref, out_ref in ((0, mine_ref, own_ref), (2 * half, other_ref, send_ref)):
        targets = targets_ref[start : start + 2 * half, :]
        field = product(targets, low_ref, mass_ref, 0, total, features)
        field += product(targets, high_ref, mass_ref, 0, total, features, total)
        out_ref[...] = field.astype(out_ref.dtype)


def final_kernel(count, features, near_ref, interp_ref, sv_ref, own_ref, got_ref, *refs):
    packs, (out_ref, low_ref, high_ref, mass_ref) = refs[:count], refs[count:]
    half = packs[0].shape[0] // 3
    skeleton_half = sv_ref.shape[0] // 3
    total = count * half
    for position, pack in enumerate(packs):
        rows = slice(position * half, (position + 1) * half)
        later = slice(total + position * half, total + (position + 1) * half)
        low, high = extended_halves(pack[2 * half :, :], features, False)
        low_ref[rows, :] = low
        high_ref[rows, :] = high
        mass_ref[rows, :] = pack[:half, :]
        mass_ref[later, :] = pack[half : 2 * half, :]
    targets = jnp.concatenate(extended_halves(sv_ref[:skeleton_half, :], features, True), axis=0)
    field = own_ref[...] + got_ref[...].astype(F32)
    field += product(targets, low_ref, mass_ref, 0, total, features)
    field += product(targets, high_ref, mass_ref, 0, total, features, total)
    coarse = field.astype(BF16)
    out_ref[...] = (near_ref[...] + dot_nn(interp_ref[...], coarse)).astype(out_ref.dtype)


def on_device(points, weights, interp, cluster_interp, skeleton_rows, near_flags, cluster_rows):
    leaves, groups = lax.axis_size("leaf"), lax.axis_size("group")
    leaf_points, features = points.shape
    columns = weights.shape[1]
    skeletons = interp.shape[1]
    cluster_count, picked = cluster_rows.shape
    members = leaves // cluster_count
    core_mask, chip_mask, reduced = 1, 2, 4
    half, sk_half, part = leaf_points // 2, skeletons // 2, picked // 2
    sum_rows = part + part // 2
    flags = (near_flags,)
    tile_flops = 2 * leaf_points * leaf_points * (2 * features + columns)

    (halo,) = call(pack_kernel, [((half + leaf_points, columns), BF16)], [points, weights], moved=10**6)
    halo_beside = xor_exchange(halo, "leaf", chip_mask)
    halo_core = xor_exchange(halo, "leaf", core_mask)

    skeleton, cluster_sum, cluster_send = call(
        skeleton_kernel,
        [((sk_half * 3, columns), BF16), ((sum_rows, columns), F32), ((sum_rows, columns), BF16)],
        [points, weights, interp, cluster_interp, skeleton_rows, cluster_rows],
        scratch=[((picked, columns), F32), ((part, columns), F32)],
        flops=4 * leaf_points * skeletons * columns,
        moved=2 * 10**6,
    )

    pieces = {0: skeleton}
    mask = leaves // 2
    while mask >= 1:
        if mask != reduced:
            for known in sorted(pieces):
                pieces[known | mask] = xor_exchange(pieces[known], "leaf", mask)
        mask //= 2

    got = xor_exchange(cluster_send, "leaf", core_mask)
    cluster_sum, cluster_send = call(
        first_add_kernel,
        [((sum_rows, columns), F32), ((sum_rows + sk_half + 16, columns), BF16)],
        [flags, cluster_sum, got, skeleton],
        moved=10**6,
    )
    partner = got = xor_exchange(cluster_send, "leaf", reduced)
    mask = chip_mask
    while mask < members:
        if mask != reduced:
            cluster_sum, cluster_send = call(
                add_kernel,
                [((sum_rows, columns), F32), ((sum_rows, columns), BF16)],
                [cluster_sum, got],
                moved=10**6,
            )
            got = xor_exchange(cluster_send, "leaf", mask)
        mask *= 2
    cluster_sum, cluster_send = call(
        add_kernel,
        [((sum_rows, columns), F32), ((sum_rows, columns), BF16)],
        [cluster_sum, got],
        moved=10**6,
    )
    own_group = [cluster_send]
    while mask < leaves:
        own_group += [xor_exchange(pack, "leaf", mask) for pack in own_group]
        mask *= 2
    packs = []
    for shift in range(1, groups):
        pairs = [(i, (i + shift) % groups) for i in range(groups)]
        packs += [lax.ppermute(pack, "group", pairs) for pack in own_group]
    packs += [xor_exchange(pack, "leaf", core_mask) for pack in packs]

    near_outs = ((leaf_points, columns), F32)
    tile_scratch = [((leaf_points, columns), BF16)]
    targets, near = call(
        functools.partial(near_kernel, 0, features),
        [((leaf_points, columns), BF16), near_outs],
        [flags, halo, halo_core],
        scratch=tile_scratch,
        flops=2 * tile_flops,
        moved=3 * 10**6,
    )
    near_step = functools.partial(
        call, outs=[near_outs], scratch=tile_scratch, flops=3 * tile_flops // 2, moved=3 * 10**6
    )
    halo_across = xor_exchange(halo_beside, "leaf", core_mask)
    (near,) = near_step(
        functools.partial(near_kernel, 1, features),
        ins=[flags, halo_beside, halo_across, targets, near],
    )
    ahead = [(i, i + 4) for i in range(leaves - 4) if i & chip_mask == 0]
    behind = [(i, i - 4) for i in range(4, leaves) if i & chip_mask != 0]
    halo_far = lax.ppermute(halo_beside, "leaf", ahead + behind)
    halo_far_across = xor_exchange(halo_far, "leaf", core_mask)
    (near,) = near_step(
        functools.partial(near_kernel, 2, features),
        ins=[flags, halo_far, halo_far_across, targets, near],
    )

    masks = sorted(pieces)
    sources = len(masks) * sk_half
    field, field_send = call(
        functools.partial(sibling_kernel, masks, reduced, features),
        [((skeletons, columns), F32), ((skeletons, columns), BF16)],
        [flags, partner] + [pieces[m] for m in masks],
        scratch=[((sources, columns), BF16)] * 2
        + [((2 * sources, columns), BF16)] * 2
        + [((2 * skeletons, columns), BF16)],
        flops=4 * skeletons * 2 * sources * (2 * features + columns),
        moved=2 * 10**6,
    )
    field_got = xor_exchange(field_send, "leaf", reduced)

    sources = len(packs) * (part // 2)
    (potential,) = call(
        functools.partial(final_kernel, len(packs), features),
        [((leaf_points, columns), BF16)],
        [near, interp, skeleton, field, field_got] + packs,
        scratch=[((sources, columns), BF16)] * 2 + [((2 * sources, columns), BF16)],
        flops=2 * skeletons * 2 * sources * (2 * features + columns),
        moved=2 * 10**6,
    )
    return potential


def solution(mesh):
    placed = (P(("group", "leaf"), None),) * 6 + (P("group", None),)
    return jax.shard_map(
        on_device, mesh=mesh, in_specs=placed, out_specs=P(("group", "leaf"), None), check_vma=False
    )
```

```python
import functools
import math

import jax
import jax.numpy as jnp
from jax import lax
from jax.experimental import pallas as pl
from jax.experimental.pallas import tpu as pltpu
from jax.sharding import PartitionSpec as P

BF16 = jnp.bfloat16
F32 = jnp.float32
VMEM_BYTES = 24 * 1024 * 1024
TARGET_ROWS = 256
SOURCE_ROWS = 512


def vmem():
    return pl.BlockSpec(memory_space=pltpu.VMEM)


def call(body, outs, ins, scratch=(), after=(), flops=0, moved=0):
    waits = len(after)
    return pl.pallas_call(
        lambda *refs: body(*refs[waits:]),
        out_shape=[jax.ShapeDtypeStruct(shape, dtype) for shape, dtype in outs],
        in_specs=[pl.BlockSpec(memory_space=pl.ANY) for _ in after] + [vmem() for _ in ins],
        out_specs=[vmem() for _ in outs],
        scratch_shapes=[pltpu.VMEM(shape, dtype) for shape, dtype in scratch],
        compiler_params=pltpu.CompilerParams(vmem_limit_bytes=VMEM_BYTES),
        cost_estimate=pl.CostEstimate(flops=flops, bytes_accessed=moved, transcendentals=0),
    )(*after, *ins)


def hand_on(value, *after):
    anywhere = pl.BlockSpec(memory_space=pl.ANY)
    return pl.pallas_call(
        lambda *refs: None,
        out_shape=jax.ShapeDtypeStruct(value.shape, value.dtype),
        in_specs=[anywhere] * (1 + len(after)),
        out_specs=anywhere,
        input_output_aliases={0: 0},
        cost_estimate=pl.CostEstimate(flops=0, bytes_accessed=0, transcendentals=0),
    )(value, *after)


def dot_nt(a, b):
    return lax.dot_general(a, b, (((1,), (1,)), ((), ())), preferred_element_type=F32)


def dot_tn(a, b):
    return lax.dot_general(a, b, (((0,), (0,)), ((), ())), preferred_element_type=F32)


def dot_nn(a, b):
    return jnp.dot(a, b, preferred_element_type=F32)


def pack_halves(values):
    half = values.shape[0] // 2
    return jnp.concatenate([values[:half], values[half:]], axis=1)


def extended(values, features, as_target):
    lane = lax.broadcasted_iota(jnp.int32, values.shape, 1)
    kept = jnp.where(lane < features, values, 0.0)
    norm = -0.5 * jnp.sum(kept * kept, axis=1, keepdims=True)
    high = norm.astype(BF16).astype(F32)
    rest = norm - high
    middle = rest.astype(BF16).astype(F32)
    low = rest - middle
    first = features if as_target else features + 3
    ones = features + 3 if as_target else features
    out = jnp.where((lane >= ones) & (lane < ones + 3), 1.0, kept)
    out = jnp.where(lane == first, high, out)
    out = jnp.where(lane == first + 1, middle, out)
    out = jnp.where(lane == first + 2, low, out)
    return out.astype(BF16)


def extended_halves(packed, features, as_target):
    wide = packed.astype(F32)
    return (
        extended(wide, features, as_target),
        extended(pltpu.roll(wide, features, 1), features, as_target),
    )


def exponent_scale(features):
    return 4.0 / features * math.log2(math.e)


def kernel_values(targets, sources, features):
    return jnp.exp2(dot_nt(targets, sources) * exponent_scale(features)).astype(BF16)


def product(targets, source_ref, mass_ref, first, rows, features, mass_first=0):
    total = None
    step = min(SOURCE_ROWS, rows)
    for start in range(0, rows, step):
        tile = kernel_values(targets, source_ref[first + start : first + start + step, :], features)
        term = dot_nn(tile, mass_ref[mass_first + start : mass_first + start + step, :])
        total = term if total is None else total + term
    return total


def xor_exchange(value, axis, mask):
    return lax.ppermute(value, axis, [(i, i ^ mask) for i in range(lax.axis_size(axis))])


def pack_kernel(points_ref, weights_ref, halo_ref):
    features, rows = points_ref.shape
    half = rows // 2
    spread = (features, 2 * features)
    row = lax.broadcasted_iota(jnp.int32, spread, 0)
    lane = lax.broadcasted_iota(jnp.int32, spread, 1)
    left = (row == lane).astype(F32).astype(BF16)
    right = (row + features == lane).astype(F32).astype(BF16)
    packed = dot_tn(points_ref[:, :half], left) + dot_tn(points_ref[:, half:], right)
    halo_ref[:half, :] = packed.astype(BF16)
    halo_ref[half:, :] = weights_ref[...]


def flag_of(flags_ref, distance):
    columns = flags_ref.shape[1]
    lane = lax.broadcasted_iota(jnp.int32, (1, columns), 1)
    here = lane == distance + (columns - 1) // 2
    return jnp.sum(jnp.where(here, flags_ref[...], 0).astype(F32), axis=1, keepdims=True)


def skeleton_kernel(
    points_ref, weights_ref, interp_ref, ci_ref, rows_ref, ids_ref, sv_ref, sum_ref, send_ref, u_ref, c_ref
):
    leaf = lax.axis_index("leaf")
    points, skeleton_count = points_ref.shape[1], interp_ref.shape[1]
    cluster_count, picked = ids_ref.shape
    members = lax.axis_size("leaf") // cluster_count
    core = leaf % 2
    one = (
        lax.broadcasted_iota(jnp.int32, (points, skeleton_count), 0) == rows_ref[...]
    ).astype(F32).astype(BF16)
    skeleton = lax.dot_general(one, points_ref[...], (((0,), (1,)), ((), ())), preferred_element_type=F32)
    charges = dot_tn(interp_ref[...], weights_ref[...]).astype(BF16)
    half = skeleton_count // 2
    sv_ref[:half, :] = pack_halves(skeleton).astype(BF16)
    sv_ref[half:, :] = charges
    u_ref[...] = dot_tn(ci_ref[...], charges)
    ids = ids_ref[pl.ds(leaf // members, 1), :] - (leaf % members) * skeleton_count
    chosen = (
        lax.broadcasted_iota(jnp.int32, (skeleton_count, picked), 0) == ids
    ).astype(F32).astype(BF16)
    cluster = dot_tn(chosen, skeleton.astype(BF16))
    part = picked // 2
    c_ref[: part // 2, :] = pack_halves(cluster[:part])
    c_ref[part // 2 :, :] = pack_halves(cluster[part:])
    sum_ref[:part, :] = u_ref[pl.ds(core * part, part), :]
    sum_ref[part:, :] = c_ref[pl.ds(core * (part // 2), part // 2), :]
    send_ref[:part, :] = u_ref[pl.ds((1 - core) * part, part), :].astype(BF16)
    send_ref[part:, :] = c_ref[pl.ds((1 - core) * (part // 2), part // 2), :].astype(BF16)


def first_add_kernel(flags_ref, sum_ref, got_ref, sv_ref, new_ref, send_ref):
    rows = sum_ref.shape[0]
    half = send_ref.shape[0] - 16 - rows
    total = sum_ref[...] + got_ref[...].astype(F32)
    new_ref[...] = total
    send_ref[:rows, :] = total.astype(BF16)
    send_ref[rows : rows + half, :] = sv_ref[:half, :]
    columns = flags_ref.shape[1]
    row = lax.broadcasted_iota(jnp.int32, (columns, send_ref.shape[1]), 0)
    lane = lax.broadcasted_iota(jnp.int32, (columns, send_ref.shape[1]), 1)
    spread = dot_nn(flags_ref[...].astype(F32), (row == lane).astype(F32))
    send_ref[rows + half :, :] = jnp.broadcast_to(spread, (16, send_ref.shape[1])).astype(BF16)


def add_kernel(sum_ref, got_ref, new_ref, send_ref):
    rows = sum_ref.shape[0]
    total = sum_ref[...] + got_ref[:rows, :].astype(F32)
    new_ref[...] = total
    send_ref[...] = total.astype(BF16)


def near_tile(targets_ref, halo_ref, source_ref, near_ref, flag, features):
    half = source_ref.shape[0] // 2
    low, high = extended_halves(halo_ref[:half, :], features, False)
    source_ref[:half, :] = low
    source_ref[half:, :] = high
    for start in range(0, targets_ref.shape[0], TARGET_ROWS):
        rows = slice(start, start + TARGET_ROWS)
        near_ref[rows, :] += flag * product(
            targets_ref[rows, :], source_ref, halo_ref, 0, 2 * half, features, half
        )


def near_kernel(stage, features, flags_ref, own_ref, across_ref, *refs):
    leaf = lax.axis_index("leaf")
    core, chip = leaf % 2, (leaf // 2) % 2
    side, beside = 1 - 2 * core, 1 - 2 * chip
    if stage == 0:
        targets_ref, near_ref, source_ref = refs
        half = targets_ref.shape[0] // 2
        low, high = extended_halves(own_ref[:half, :], features, True)
        targets_ref[:half, :] = low
        targets_ref[half:, :] = high
        near_ref[...] = jnp.zeros_like(near_ref)
        distances = (0, side)
    else:
        targets_ref, before_ref, near_ref, source_ref = refs
        near_ref[...] = before_ref[...]
        distances = (2 * beside if stage == 1 else -2 * beside, -side)
    near_tile(targets_ref, own_ref, source_ref, near_ref, flag_of(flags_ref, distances[0]), features)

    def second():
        flag = flag_of(flags_ref, distances[1])
        near_tile(targets_ref, across_ref, source_ref, near_ref, flag, features)

    if stage == 0:
        second()
    else:
        pl.when(core != chip if stage == 1 else core == chip)(second)


def join_kernel(first_ref, second_ref, both_ref):
    rows = first_ref.shape[0]
    both_ref[:rows, :] = first_ref[...]
    both_ref[rows:, :] = second_ref[...]


def sibling_kernel(masks, reduced, features, skeletons, flags_ref, got_ref, *refs):
    pieces, refs = refs[: len(masks)], refs[len(masks) :]
    own_ref, send_ref, low_ref, high_ref, mine_ref, other_ref, targets_ref = refs
    leaf = lax.axis_index("leaf")
    reach = (flags_ref.shape[1] - 1) // 2
    half = skeletons // 2
    got_rows = got_ref.shape[0]
    other_points = got_ref[got_rows - 16 - half : got_rows - 16, :]
    other_flags = got_ref[got_rows - 16 :, :].astype(F32)[:1, :]
    lane = lax.broadcasted_iota(jnp.int32, other_flags.shape, 1)
    flat = [(m, piece, 3 * half * i) for part, piece in zip(masks, pieces) for i, m in enumerate(part)]
    total = len(flat) * half
    for position, (mask, piece, start) in enumerate(flat):
        source = leaf ^ mask
        rows = slice(position * half, (position + 1) * half)
        later = slice(total + position * half, total + (position + 1) * half)
        low, high = extended_halves(piece[start : start + half, :], features, False)
        low_ref[rows, :] = low
        high_ref[rows, :] = high
        kept = 1.0 - flag_of(flags_ref, source - leaf)
        flagged = jnp.where(lane == source - (leaf ^ reduced) + reach, other_flags, 0.0)
        kept_other = 1.0 - jnp.sum(flagged, axis=1, keepdims=True)
        mass = piece[start + half : start + 3 * half, :].astype(F32)
        for ref, factor in ((mine_ref, kept), (other_ref, kept_other)):
            scaled = (mass * factor).astype(BF16)
            ref[rows, :] = scaled[:half]
            ref[later, :] = scaled[half:]
    for start, packed in ((0, pieces[0][:half, :]), (2 * half, other_points)):
        low, high = extended_halves(packed, features, True)
        targets_ref[start : start + half, :] = low
        targets_ref[start + half : start + 2 * half, :] = high
    for start, mass_ref, out_ref in ((0, mine_ref, own_ref), (2 * half, other_ref, send_ref)):
        targets = targets_ref[start : start + 2 * half, :]
        field = product(targets, low_ref, mass_ref, 0, total, features)
        field += product(targets, high_ref, mass_ref, 0, total, features, total)
        out_ref[...] = field.astype(out_ref.dtype)


def final_kernel(count, features, near_ref, interp_ref, sv_ref, own_ref, got_ref, *refs):
    packs, (out_ref, low_ref, high_ref, mass_ref) = refs[:count], refs[count:]
    half = packs[0].shape[0] // 3
    skeleton_half = sv_ref.shape[0] // 3
    total = count * half
    for position, pack in enumerate(packs):
        rows = slice(position * half, (position + 1) * half)
        later = slice(total + position * half, total + (position + 1) * half)
        low, high = extended_halves(pack[2 * half :, :], features, False)
        low_ref[rows, :] = low
        high_ref[rows, :] = high
        mass_ref[rows, :] = pack[:half, :]
        mass_ref[later, :] = pack[half : 2 * half, :]
    targets = jnp.concatenate(extended_halves(sv_ref[:skeleton_half, :], features, True), axis=0)
    field = own_ref[...] + got_ref[...].astype(F32)
    field += product(targets, low_ref, mass_ref, 0, total, features)
    field += product(targets, high_ref, mass_ref, 0, total, features, total)
    coarse = field.astype(BF16)
    out_ref[...] = (near_ref[...] + dot_nn(interp_ref[...], coarse)).astype(out_ref.dtype)


def on_device(points, weights, interp, cluster_interp, skeleton_rows, near_flags, cluster_rows):
    leaves, groups = lax.axis_size("leaf"), lax.axis_size("group")
    leaf_points, features = points.shape
    columns = weights.shape[1]
    skeletons = interp.shape[1]
    cluster_count, picked = cluster_rows.shape
    members = leaves // cluster_count
    core_mask, chip_mask, reduced = 1, 2, 4
    half, sk_half, part = leaf_points // 2, skeletons // 2, picked // 2
    sum_rows = part + part // 2
    flags, turned = near_flags, points.T
    tile_flops = 2 * leaf_points * leaf_points * (2 * features + columns)

    (halo,) = call(pack_kernel, [((half + leaf_points, columns), BF16)], [turned, weights], moved=10**6)
    halo_beside = xor_exchange(halo, "leaf", chip_mask)
    halo_core = xor_exchange(halo, "leaf", core_mask)

    skeleton, cluster_sum, cluster_send = call(
        skeleton_kernel,
        [((sk_half * 3, columns), BF16), ((sum_rows, columns), F32), ((sum_rows, columns), BF16)],
        [turned, weights, interp, cluster_interp, skeleton_rows, cluster_rows],
        scratch=[((picked, columns), F32), ((part, columns), F32)],
        after=[halo],
        flops=4 * leaf_points * skeletons * columns,
        moved=2 * 10**6,
    )

    sum_outs = [((sum_rows, columns), F32), ((sum_rows, columns), BF16)]
    got = xor_exchange(cluster_send, "leaf", core_mask)
    gathered, masks = skeleton, [0]
    gather_masks = [1 << i for i in reversed(range(1, leaves.bit_length() - 1)) if 1 << i != reduced]
    last_mask = gather_masks.pop()
    first_got = xor_exchange(gathered, "leaf", gather_masks[0]) if gather_masks else None
    cluster_sum, cluster_send = call(
        first_add_kernel,
        [sum_outs[0], ((sum_rows + sk_half + 16, columns), BF16)],
        [flags, cluster_sum, got, skeleton],
        moved=10**6,
    )
    partner = got = xor_exchange(cluster_send, "leaf", reduced)

    near_outs = ((leaf_points, columns), F32)
    tile_scratch = [((leaf_points, columns), BF16)]
    targets, near = call(
        functools.partial(near_kernel, 0, features),
        [((leaf_points, columns), BF16), near_outs],
        [flags, halo, halo_core],
        scratch=tile_scratch,
        after=[cluster_send],
        flops=2 * tile_flops,
        moved=3 * 10**6,
    )
    near_step = functools.partial(
        call, outs=[near_outs], scratch=tile_scratch, flops=3 * tile_flops // 2, moved=3 * 10**6
    )

    add_masks = [1 << i for i in range(1, members.bit_length() - 1) if 1 << i != reduced]
    cluster_sum, cluster_send = call(add_kernel, sum_outs, [cluster_sum, got], after=[near], moved=10**6)
    got = xor_exchange(cluster_send, "leaf", add_masks[0])

    halo_beside = hand_on(halo_beside, cluster_send)
    ahead = [(i, i + 4) for i in range(leaves - 4) if i & chip_mask == 0]
    behind = [(i, i - 4) for i in range(4, leaves) if i & chip_mask != 0]
    halo_far = lax.ppermute(halo_beside, "leaf", ahead + behind)
    halo_across = xor_exchange(halo_beside, "leaf", core_mask)

    for mask in gather_masks:
        arrived = first_got if mask == gather_masks[0] else xor_exchange(gathered, "leaf", mask)
        masks = masks + [m | mask for m in masks]
        (gathered,) = call(
            join_kernel, [((2 * gathered.shape[0], columns), BF16)], [gathered, arrived], moved=10**6
        )
    pieces = [(masks, gathered), ([m | last_mask for m in masks], xor_exchange(gathered, "leaf", last_mask))]
    pieces += [([m | core_mask for m in part], xor_exchange(piece, "leaf", core_mask)) for part, piece in pieces]

    for mask in add_masks[1:]:
        cluster_sum, cluster_send = call(
            add_kernel, sum_outs, [cluster_sum, got], after=[gathered], moved=10**6
        )
        got = xor_exchange(cluster_send, "leaf", mask)

    (near,) = near_step(
        functools.partial(near_kernel, 1, features),
        ins=[flags, halo_beside, halo_across, targets, near],
        after=[cluster_send],
    )

    sources = 2 * len(pieces[0][0]) * 2 * sk_half
    field, field_send = call(
        functools.partial(sibling_kernel, [p for p, _ in pieces], reduced, features, skeletons),
        [((skeletons, columns), F32), ((skeletons, columns), BF16)],
        [flags, partner] + [piece for _, piece in pieces],
        scratch=[((sources, columns), BF16)] * 2
        + [((2 * sources, columns), BF16)] * 2
        + [((2 * skeletons, columns), BF16)],
        after=[near],
        flops=4 * skeletons * 2 * sources * (2 * features + columns),
        moved=2 * 10**6,
    )
    field_got = xor_exchange(field_send, "leaf", reduced)

    cluster_sum, cluster_send = call(add_kernel, sum_outs, [cluster_sum, got], after=[field], moved=10**6)
    own_group = [cluster_send]
    mask = members
    while mask < leaves:
        own_group += [xor_exchange(pack, "leaf", mask) for pack in own_group]
        mask *= 2
    packs = []
    for shift in range(1, groups):
        pairs = [(i, (i + shift) % groups) for i in range(groups)]
        packs += [lax.ppermute(pack, "group", pairs) for pack in own_group]
    packs += [xor_exchange(pack, "leaf", core_mask) for pack in packs]

    halo_far_across = xor_exchange(halo_far, "leaf", core_mask)
    (near,) = near_step(
        functools.partial(near_kernel, 2, features),
        ins=[flags, halo_far, halo_far_across, targets, near],
        after=[cluster_send],
    )

    sources = len(packs) * (part // 2)
    (potential,) = call(
        functools.partial(final_kernel, len(packs), features),
        [((leaf_points, columns), BF16)],
        [near, interp, skeleton, field, field_got] + packs,
        scratch=[((sources, columns), BF16)] * 2 + [((2 * sources, columns), BF16)],
        flops=2 * skeletons * 2 * sources * (2 * features + columns),
        moved=2 * 10**6,
    )
    return potential


def solution(mesh):
    placed = (P(("group", "leaf"), None),) * 6 + (P("group", None),)
    return jax.shard_map(
        on_device, mesh=mesh, in_specs=placed, out_specs=P(("group", "leaf"), None), check_vma=False
    )
```

```python
import functools
import math

import jax
import jax.numpy as jnp
from jax import lax
from jax.experimental import pallas as pl
from jax.experimental.pallas import tpu as pltpu
from jax.sharding import PartitionSpec as P

BF16 = jnp.bfloat16
F32 = jnp.float32
VMEM_BYTES = 24 * 1024 * 1024
LANES = 128
TARGET_ROWS = 512
SOURCE_ROWS = 512
WORK = {
    "prepare": 10**6,
    "first_add": 10**6,
    "near_self": 2 * 10**9,
    "near_core": 2 * 10**9,
    "add_a": 10**6,
    "near_beside": 2 * 10**9,
    "add_b": 10**6,
    "near_across": 2 * 10**9,
    "add_c": 10**6,
    "sibling": 2 * 10**9,
    "near_far": 2 * 10**9,
    "near_last": 2 * 10**9,
    "final": 2 * 10**9,
}


def vmem():
    return pl.BlockSpec(memory_space=pltpu.VMEM)


def call(body, outs, ins, scratch=(), after=(), in_place=False, work=10**6):
    waits = len(after)
    return pl.pallas_call(
        lambda *refs: body(*refs[waits:]),
        out_shape=[jax.ShapeDtypeStruct(shape, dtype) for shape, dtype in outs],
        in_specs=[pl.BlockSpec(memory_space=pl.ANY) for _ in after] + [vmem() for _ in ins],
        out_specs=[vmem() for _ in outs],
        scratch_shapes=[pltpu.VMEM(shape, dtype) for shape, dtype in scratch],
        input_output_aliases={waits: 0} if in_place else {},
        compiler_params=pltpu.CompilerParams(vmem_limit_bytes=VMEM_BYTES),
        cost_estimate=pl.CostEstimate(flops=work, bytes_accessed=0, transcendentals=0),
    )(*after, *ins)


def hand_on(value, *after):
    return pl.pallas_call(
        lambda *refs: None,
        out_shape=jax.ShapeDtypeStruct(value.shape, value.dtype),
        in_specs=[vmem()] + [pl.BlockSpec(memory_space=pl.ANY) for _ in after],
        out_specs=vmem(),
        input_output_aliases={0: 0},
        compiler_params=pltpu.CompilerParams(vmem_limit_bytes=VMEM_BYTES),
        cost_estimate=pl.CostEstimate(flops=0, bytes_accessed=0, transcendentals=0),
    )(value, *after)


def dot_nt(a, b):
    return lax.dot_general(a, b, (((1,), (1,)), ((), ())), preferred_element_type=F32)


def dot_nn(a, b):
    return jnp.dot(a, b, preferred_element_type=F32)


def xor_exchange(value, axis, mask):
    return lax.ppermute(value, axis, [(i, i ^ mask) for i in range(lax.axis_size(axis))])


def up16(rows):
    return -(-rows // 16) * 16


def norm_rows(points):
    return up16(3 * points // LANES)


def scale_of(features):
    return 4.0 / features * math.log2(math.e)


def three_parts(values):
    high = values.astype(BF16).astype(F32)
    rest = values - high
    middle = rest.astype(BF16).astype(F32)
    return high, middle, rest - middle


def norm_block(norms):
    count = norms.shape[1] // LANES
    parts = [
        part[:, i * LANES : (i + 1) * LANES] for part in three_parts(norms) for i in range(count)
    ]
    rest = norm_rows(norms.shape[1]) - len(parts)
    return jnp.concatenate(parts + [jnp.zeros((rest, LANES), F32)], axis=0)


def source_norms(block, points):
    count = points // LANES
    block = block.astype(F32)
    rows = block[:count] + block[count : 2 * count] + block[2 * count : 3 * count]
    return tuple(
        jnp.concatenate([rows[i : i + 1] for i in range(h * count // 2, (h + 1) * count // 2)], axis=1)
        for h in range(2)
    )


def target_forms(packed, features):
    wide = packed.astype(F32)
    turned = pltpu.roll(wide, features, 1)
    lane = lax.broadcasted_iota(jnp.int32, wide.shape, 1)
    low, high, norms = [], [], []
    for first, second in ((wide, turned), (turned, wide)):
        kept = jnp.where(lane < features, first, 0.0)
        low.append(kept)
        high.append(jnp.where(lane >= features, second, 0.0))
        parts = three_parts(-0.5 * jnp.sum(kept * kept, axis=1, keepdims=True))
        norms.append(
            jnp.where(lane == 0, parts[0], jnp.where(lane == 1, parts[1], jnp.where(lane == 2, parts[2], 0.0)))
        )
    return tuple(jnp.concatenate(form, axis=0).astype(BF16) for form in (low, high, norms))


def ones_beside(packed):
    lane = lax.broadcasted_iota(jnp.int32, packed.shape, 1)
    return jnp.concatenate([packed, jnp.where(lane < 3, 1.0, 0.0).astype(BF16)], axis=1)


def kernel_values(targets, parts, sources, norms, features):
    exponent = dot_nt(jnp.concatenate([targets, parts], axis=1), sources) * scale_of(features) + norms
    return jnp.exp2(exponent).astype(BF16)


def flag_of(flags_ref, distance):
    columns = flags_ref.shape[1]
    lane = lax.broadcasted_iota(jnp.int32, (1, columns), 1)
    here = lane == distance + (columns - 1) // 2
    return jnp.sum(jnp.where(here, flags_ref[...], 0).astype(F32), axis=1, keepdims=True)


def prepare_kernel(
    points_hbm, weights_hbm, interp_hbm, ci_hbm, rows_hbm, flags_hbm, ids_hbm,
    halo_ref, sv_ref, sum_ref, send_ref, flags_ref,
    points_ref, interp_ref, ci_ref, rows_ref, ids_ref, all_ref, arrived,
):
    features, points = points_ref.shape
    half, skeletons = points // 2, interp_ref.shape[1]
    pairs = (
        (rows_hbm, rows_ref),
        (points_hbm, points_ref),
        (weights_hbm, halo_ref.at[pl.ds(half, points)]),
        (interp_hbm, interp_ref),
        (ids_hbm, ids_ref),
        (ci_hbm, ci_ref),
        (flags_hbm, flags_ref),
    )
    copies = [pltpu.make_async_copy(source, place, arrived.at[i]) for i, (source, place) in enumerate(pairs)]
    for copy in copies:
        copy.start()
    leaf = lax.axis_index("leaf")
    core = leaf % 2
    cluster_count, picked = ids_ref.shape
    members = lax.axis_size("leaf") // cluster_count
    source_scale = -0.5 * scale_of(features)

    def packed(turned):
        n = turned.shape[1]
        return jnp.concatenate([turned[:, : n // 2], turned[:, n // 2 :]], axis=0).T

    def norms(turned):
        return source_scale * jnp.sum(turned * turned, axis=0, keepdims=True)

    copies[0].wait()
    one = (
        lax.broadcasted_iota(jnp.int32, (points, skeletons), 0) == rows_ref[...]
    ).astype(F32).astype(BF16)
    copies[1].wait()
    skeleton = dot_nn(points_ref[...], one)
    copies[2].wait()
    weights_turned = halo_ref[half : half + points, :].astype(F32).T.astype(BF16)
    copies[3].wait()
    charges_turned = dot_nn(weights_turned, interp_ref[...]).astype(BF16)
    copies[4].wait()
    ids = ids_ref[pl.ds(leaf // members, 1), :] - (leaf % members) * skeletons
    chosen = (
        lax.broadcasted_iota(jnp.int32, (skeletons, picked), 0) == ids
    ).astype(F32).astype(BF16)
    cluster = dot_nn(skeleton.astype(BF16), chosen)
    copies[5].wait()
    sums = dot_nn(charges_turned, ci_ref[...]).T
    part = picked // 2
    rows = sum_ref.shape[0]
    for h in range(2):
        columns = slice(h * part, (h + 1) * part)
        place = slice(h * rows, h * rows + part)
        all_ref[place, :] = sums[columns]
        place = slice(h * rows + part, h * rows + part + part // 2)
        all_ref[place, :] = packed(cluster[:, columns])
        place = slice(h * rows + part + part // 2, (h + 1) * rows)
        all_ref[place, :] = norm_block(norms(cluster[:, columns]))
    sum_ref[...] = all_ref[pl.ds(core * rows, rows), :]
    send_ref[...] = all_ref[pl.ds((1 - core) * rows, rows), :].astype(BF16)
    sk_half, sk_norms = skeletons // 2, norm_rows(skeletons)
    sv_ref[:sk_half, :] = packed(skeleton).astype(BF16)
    sv_ref[sk_half : sk_half + sk_norms, :] = norm_block(norms(skeleton)).astype(BF16)
    sv_ref[sk_half + sk_norms :, :] = charges_turned.astype(F32).T.astype(BF16)
    wide = points_ref[...].astype(F32)
    halo_ref[:half, :] = packed(wide).astype(BF16)
    halo_ref[half + points :, :] = norm_block(norms(wide)).astype(BF16)
    copies[6].wait()


def add_kernel(with_skeleton, last, sum_ref, got_ref, *refs):
    rows = sum_ref.shape[0]
    total = sum_ref[...] + got_ref[:rows, :].astype(F32)
    if with_skeleton:
        flags_ref, sv_ref, *refs = refs
        send_ref = refs[0]
        points = send_ref.shape[0] - 16 - rows
        send_ref[rows : rows + points, :] = sv_ref[:points, :]
        columns = flags_ref.shape[1]
        row = lax.broadcasted_iota(jnp.int32, (columns, LANES), 0)
        lane = lax.broadcasted_iota(jnp.int32, (columns, LANES), 1)
        spread = dot_nn(flags_ref[...].astype(F32), (row == lane).astype(F32))
        send_ref[rows + points :, :] = jnp.broadcast_to(spread, (16, LANES)).astype(BF16)
    refs[0][:rows, :] = total.astype(BF16)
    if not last:
        refs[1][...] = total


def near_kernel(stage, across, features, *refs):
    leaf = lax.axis_index("leaf")
    core, chip = leaf % 2, (leaf // 2) % 2
    side, beside = 1 - 2 * core, 1 - 2 * chip
    first = stage == 0 and not across
    if first:
        flags_ref, halo_ref, low_ref, high_ref, parts_ref, near_ref = refs
        half = near_ref.shape[0] // 2
        forms = target_forms(halo_ref[:half, :], features)
        for ref, form in zip((low_ref, high_ref, parts_ref), forms):
            ref[...] = form
        distance = 0
    else:
        before_ref, flags_ref, halo_ref, low_ref, high_ref, parts_ref, near_ref = refs
        half = near_ref.shape[0] // 2
        if across:
            distance = side if stage == 0 else -side
        else:
            distance = 2 * beside if stage == 1 else -2 * beside

    def tile():
        flag = flag_of(flags_ref, distance)
        norms = source_norms(halo_ref[3 * half :, :], 2 * half)
        step = min(SOURCE_ROWS, half)
        for start in range(0, 2 * half, TARGET_ROWS):
            rows = slice(start, min(start + TARGET_ROWS, 2 * half))
            total = None
            for place in range(0, half, step):
                sources = ones_beside(halo_ref[place : place + step, :])
                for h, ref in enumerate((low_ref, high_ref)):
                    terms = norms[h][:, place : place + step]
                    values = kernel_values(ref[rows, :], parts_ref[rows, :], sources, terms, features)
                    mass = halo_ref[(h + 1) * half + place : (h + 1) * half + place + step, :]
                    term = dot_nn(values, mass)
                    total = term if total is None else total + term
            near_ref[rows, :] = flag * total if first else before_ref[rows, :] + flag * total

    if across and stage > 0:
        pl.when(core != chip if stage == 1 else core == chip)(tile)
    else:
        tile()


def grouped(count, rows):
    step = max(1, SOURCE_ROWS // rows)
    return [range(i, min(i + step, count)) for i in range(0, count, step)]


def sibling_kernel(masks, reduced, features, skeletons, flags_ref, got_ref, *refs):
    pieces, (own_ref, send_ref) = refs[: len(masks)], refs[len(masks) :]
    leaf = lax.axis_index("leaf")
    reach = (flags_ref.shape[1] - 1) // 2
    half, points = skeletons // 2, skeletons // 2 + norm_rows(skeletons)
    start = got_ref.shape[0] - 16 - points
    other_flags = got_ref[start + points :, :].astype(F32)[:1, :]
    lane = lax.broadcasted_iota(jnp.int32, other_flags.shape, 1)
    forms = zip(
        target_forms(pieces[0][:half, :], features),
        target_forms(got_ref[start : start + half, :], features),
    )
    low, high, parts = [jnp.concatenate(form, axis=0) for form in forms]
    kept = []
    for mask in masks:
        source = leaf ^ mask
        flagged = jnp.where(lane == source - (leaf ^ reduced) + reach, other_flags, 0.0)
        other = 1.0 - jnp.sum(flagged, axis=1, keepdims=True)
        kept.append((1.0 - flag_of(flags_ref, source - leaf), other))
    own = send = None
    for group in grouped(len(masks), half):
        sources = ones_beside(jnp.concatenate([pieces[i][:half, :] for i in group], axis=0))
        norms = [source_norms(pieces[i][half:points, :], skeletons) for i in group]
        for h, targets in enumerate((low, high)):
            terms = jnp.concatenate([n[h] for n in norms], axis=1)
            values = kernel_values(targets, parts, sources, terms, features)
            mass = [pieces[i][points + h * half : points + (h + 1) * half, :].astype(F32) for i in group]
            masses = [
                jnp.concatenate([m * kept[i][k] for m, i in zip(mass, group)], axis=0).astype(BF16)
                for k in range(2)
            ]
            to_own = dot_nn(values[:skeletons], masses[0])
            to_other = dot_nn(values[skeletons:], masses[1])
            own = to_own if own is None else own + to_own
            send = to_other if send is None else send + to_other
    own_ref[...] = own
    send_ref[...] = send.astype(send_ref.dtype)


def final_kernel(count, features, near_ref, interp_ref, sv_ref, own_ref, got_ref, *refs):
    packs, out_ref = refs[:count], refs[count]
    skeletons = interp_ref.shape[1]
    low, high, parts = target_forms(sv_ref[: skeletons // 2, :], features)
    half = max(r for r in range(1, packs[0].shape[0]) if 3 * r + norm_rows(2 * r) <= packs[0].shape[0])
    field = own_ref[...] + got_ref[...].astype(F32)
    for group in grouped(count, half):
        sources = ones_beside(jnp.concatenate([packs[i][2 * half : 3 * half, :] for i in group], axis=0))
        norms = [source_norms(packs[i][3 * half :, :], 2 * half) for i in group]
        for h, targets in enumerate((low, high)):
            terms = jnp.concatenate([n[h] for n in norms], axis=1)
            values = kernel_values(targets, parts, sources, terms, features)
            mass = jnp.concatenate([packs[i][h * half : (h + 1) * half, :] for i in group], axis=0)
            field += dot_nn(values, mass)
    coarse = field.astype(BF16)
    out_ref[...] = (near_ref[...] + dot_nn(interp_ref[...], coarse)).astype(out_ref.dtype)


def on_device(points, weights, interp, cluster_interp, skeleton_rows, near_flags, cluster_rows):
    leaves, groups = lax.axis_size("leaf"), lax.axis_size("group")
    leaf_points, features = points.shape
    columns = weights.shape[1]
    skeletons = interp.shape[1]
    cluster_count, picked = cluster_rows.shape
    members = leaves // cluster_count
    core_mask, chip_mask, reduced = 1, 2, 4
    half, part = leaf_points // 2, picked // 2
    sum_rows = part + part // 2 + norm_rows(part)
    sv_points = skeletons // 2 + norm_rows(skeletons)

    arguments = [points.T, weights, interp, cluster_interp, skeleton_rows, near_flags, cluster_rows]
    outs = [
        ((half + leaf_points + norm_rows(leaf_points), columns), BF16),
        ((sv_points + skeletons, columns), BF16),
        ((sum_rows, columns), F32),
        ((sum_rows, columns), BF16),
        (near_flags.shape, near_flags.dtype),
    ]
    scratch = [(x.shape, x.dtype) for x in (arguments[0], interp, cluster_interp, skeleton_rows, cluster_rows)]
    scratch += [((2 * sum_rows, columns), F32)]
    halo, skeleton, cluster_sum, cluster_send, flags = pl.pallas_call(
        prepare_kernel,
        out_shape=[jax.ShapeDtypeStruct(shape, dtype) for shape, dtype in outs],
        in_specs=[pl.BlockSpec(memory_space=pltpu.HBM) for _ in arguments],
        out_specs=[vmem() for _ in outs],
        scratch_shapes=[pltpu.VMEM(shape, dtype) for shape, dtype in scratch]
        + [pltpu.SemaphoreType.DMA((len(arguments),))],
        compiler_params=pltpu.CompilerParams(vmem_limit_bytes=VMEM_BYTES),
        cost_estimate=pl.CostEstimate(flops=WORK["prepare"], bytes_accessed=0, transcendentals=0),
    )(*[pltpu.with_memory_space_constraint(x, pltpu.HBM) for x in arguments])

    def add(name, total, got, mask, after=(), last=False):
        with_skeleton = mask == reduced
        rows = sum_rows + (sv_points + 16 if with_skeleton else 0)
        outs = [((rows, columns), BF16)] + ([] if last else [((sum_rows, columns), F32)])
        ins = [total, got] + ([flags, skeleton] if with_skeleton else [])
        body = functools.partial(add_kernel, with_skeleton, last)
        send, *total = call(body, outs, ins, after=after, work=WORK[name])
        return send, total[0] if total else None

    got = xor_exchange(cluster_send, "leaf", core_mask)
    pieces = {0: skeleton}
    pieces[chip_mask] = xor_exchange(skeleton, "leaf", chip_mask)
    pieces[core_mask] = xor_exchange(skeleton, "leaf", core_mask)
    halo_core = xor_exchange(halo, "leaf", core_mask)
    halo_beside = xor_exchange(halo, "leaf", chip_mask)
    add_masks = [1 << i for i in reversed(range(1, members.bit_length() - 1))]
    names = ["first_add", "add_a", "add_b", "add_c"]
    cluster_send, cluster_sum = add(names[0], cluster_sum, got, add_masks[0])
    got = xor_exchange(cluster_send, "leaf", add_masks[0])

    gather_masks = [1 << i for i in reversed(range(2, leaves.bit_length() - 1)) if 1 << i != reduced]
    known = [0]
    for mask in gather_masks:
        for m in list(known):
            pieces[m | mask] = xor_exchange(pieces[m], "leaf", mask)
            known.append(m | mask)
    for m in known[1:]:
        pieces[m | chip_mask] = xor_exchange(pieces[m], "leaf", chip_mask)
    for m in known:
        for n in (m, m | chip_mask):
            if n:
                pieces[n | core_mask] = xor_exchange(pieces[n], "leaf", core_mask)

    tile = ((leaf_points, columns), BF16)
    *targets, near = call(
        functools.partial(near_kernel, 0, False, features),
        [tile, tile, tile, ((leaf_points, columns), F32)],
        [flags, halo],
        after=[cluster_send],
        work=WORK["near_self"],
    )

    def near_step(name, near, stage, across, other, *after):
        return call(
            functools.partial(near_kernel, stage, across, features),
            [((leaf_points, columns), F32)],
            [near, flags, other, *targets],
            after=after,
            in_place=True,
            work=WORK[name],
        )[0]

    near = near_step("near_core", near, 0, True, halo_core)

    cluster_send, cluster_sum = add(names[1], cluster_sum, got, add_masks[1], [near])
    partner = got = xor_exchange(cluster_send, "leaf", add_masks[1])

    halo_beside = hand_on(halo_beside, cluster_send)
    ahead = [(i, i + 4) for i in range(leaves - 4) if i & chip_mask == 0]
    behind = [(i, i - 4) for i in range(4, leaves) if i & chip_mask != 0]
    halo_far = lax.ppermute(halo_beside, "leaf", ahead + behind)
    halo_across = xor_exchange(halo_beside, "leaf", core_mask)
    near = near_step("near_beside", near, 1, False, halo_beside)

    cluster_send, cluster_sum = add(names[2], cluster_sum, got, add_masks[2], [near])
    got = xor_exchange(cluster_send, "leaf", add_masks[2])
    near = near_step("near_across", near, 1, True, halo_across, cluster_send)

    cluster_send, _ = add(names[3], cluster_sum, got, 0, [near], True)
    own_group = [cluster_send]
    mask = members
    while mask < leaves:
        own_group += [xor_exchange(pack, "leaf", mask) for pack in own_group]
        mask *= 2
    packs = []
    for shift in range(1, groups):
        order = [(i, (i + shift) % groups) for i in range(groups)]
        packs += [lax.ppermute(pack, "group", order) for pack in own_group]

    masks = sorted(pieces)
    field, field_send = call(
        functools.partial(sibling_kernel, masks, reduced, features, skeletons),
        [((skeletons, columns), F32), ((skeletons, columns), BF16)],
        [flags, partner] + [pieces[m] for m in masks],
        after=[cluster_send],
        work=WORK["sibling"],
    )
    field_got = xor_exchange(field_send, "leaf", reduced)

    halo_far = hand_on(halo_far, field)
    halo_far_across = xor_exchange(halo_far, "leaf", core_mask)
    near = near_step("near_far", near, 2, False, halo_far)
    packs += [xor_exchange(pack, "leaf", core_mask) for pack in packs]
    near = near_step("near_last", near, 2, True, halo_far_across)

    (potential,) = call(
        functools.partial(final_kernel, len(packs), features),
        [((leaf_points, columns), BF16)],
        [near, interp, skeleton, field, field_got] + packs,
        work=WORK["final"],
    )
    return potential


def solution(mesh):
    placed = (P(("group", "leaf"), None),) * 6 + (P("group", None),)
    return jax.shard_map(
        on_device, mesh=mesh, in_specs=placed, out_specs=P(("group", "leaf"), None), check_vma=False
    )
```

```python
import functools
import math

import jax
import jax.numpy as jnp
from jax import lax
from jax.experimental import pallas as pl
from jax.experimental.pallas import tpu as pltpu
from jax.sharding import PartitionSpec as P

BF16 = jnp.bfloat16
F32 = jnp.float32
VMEM_BYTES = 24 * 1024 * 1024
LANES = 128
TARGET_ROWS = 512
SOURCE_ROWS = 512
ORDER = {
    "first_add": 1000000,
    "near_self": 2000000000,
    "near_core": 2000000000,
    "near_beside": 2000000000,
    "add_a": 1000000,
    "add_b": 1000000,
    "sibling": 2000000000,
    "near_across": 2000000000,
    "add_c": 1000000,
    "field": 1000000,
    "near_far": 2000000000,
    "near_last": 2000000000,
    "final": 2000000000,
}
DEADLINES = {
    "add_a": ["sv_8"],
    "sibling": ["sv_10"],
    "near_far": ["packs"],
    "near_last": ["packs_core"],
}
RELEASES = {"sv_0": "first_add", "halo_next": "add_a", "halo_far": "add_c"}


def vmem():
    return pl.BlockSpec(memory_space=pltpu.VMEM)


def call(body, outs, ins, scratch=(), after=(), in_place=False, work=10**6):
    waits = len(after)
    return pl.pallas_call(
        lambda *refs: body(*refs[waits:]),
        out_shape=[jax.ShapeDtypeStruct(shape, dtype) for shape, dtype in outs],
        in_specs=[pl.BlockSpec(memory_space=pl.ANY) for _ in after] + [vmem() for _ in ins],
        out_specs=[vmem() for _ in outs],
        scratch_shapes=[pltpu.VMEM(shape, dtype) for shape, dtype in scratch],
        input_output_aliases={waits: 0} if in_place else {},
        compiler_params=pltpu.CompilerParams(vmem_limit_bytes=VMEM_BYTES),
        cost_estimate=pl.CostEstimate(flops=work, bytes_accessed=0, transcendentals=0),
    )(*after, *ins)


def hand_on(value, *after):
    return pl.pallas_call(
        lambda *refs: None,
        out_shape=jax.ShapeDtypeStruct(value.shape, value.dtype),
        in_specs=[vmem()] + [pl.BlockSpec(memory_space=pl.ANY) for _ in after],
        out_specs=vmem(),
        input_output_aliases={0: 0},
        compiler_params=pltpu.CompilerParams(vmem_limit_bytes=VMEM_BYTES),
        cost_estimate=pl.CostEstimate(flops=0, bytes_accessed=0, transcendentals=0),
    )(value, *after)


def dot_nt(a, b):
    return lax.dot_general(a, b, (((1,), (1,)), ((), ())), preferred_element_type=F32)


def dot_nn(a, b):
    return jnp.dot(a, b, preferred_element_type=F32)


def xor_exchange(value, axis, mask):
    return lax.ppermute(value, axis, [(i, i ^ mask) for i in range(lax.axis_size(axis))])


def up16(rows):
    return -(-rows // 16) * 16


def norm_rows(points):
    return up16(3 * points // LANES)


def scale_of(features):
    return 4.0 / features * math.log2(math.e)


def three_parts(values):
    high = values.astype(BF16).astype(F32)
    rest = values - high
    middle = rest.astype(BF16).astype(F32)
    return high, middle, rest - middle


def norm_block(norms):
    count = norms.shape[1] // LANES
    parts = [
        part[:, i * LANES : (i + 1) * LANES] for part in three_parts(norms) for i in range(count)
    ]
    rest = norm_rows(norms.shape[1]) - len(parts)
    return jnp.concatenate(parts + [jnp.zeros((rest, LANES), F32)], axis=0)


def source_norms(block, points):
    count = points // LANES
    block = block.astype(F32)
    rows = block[:count] + block[count : 2 * count] + block[2 * count : 3 * count]
    return tuple(
        jnp.concatenate([rows[i : i + 1] for i in range(h * count // 2, (h + 1) * count // 2)], axis=1)
        for h in range(2)
    )


def target_forms(packed, features):
    wide = packed.astype(F32)
    turned = pltpu.roll(wide, features, 1)
    lane = lax.broadcasted_iota(jnp.int32, wide.shape, 1)
    low, high, norms = [], [], []
    for first, second in ((wide, turned), (turned, wide)):
        kept = jnp.where(lane < features, first, 0.0)
        low.append(kept)
        high.append(jnp.where(lane >= features, second, 0.0))
        parts = three_parts(-0.5 * jnp.sum(kept * kept, axis=1, keepdims=True))
        norms.append(
            jnp.where(lane == 0, parts[0], jnp.where(lane == 1, parts[1], jnp.where(lane == 2, parts[2], 0.0)))
        )
    return tuple(jnp.concatenate(form, axis=0).astype(BF16) for form in (low, high, norms))


def ones_beside(packed):
    lane = lax.broadcasted_iota(jnp.int32, packed.shape, 1)
    return jnp.concatenate([packed, jnp.where(lane < 3, 1.0, 0.0).astype(BF16)], axis=1)


def kernel_values(targets, parts, sources, norms, features):
    exponent = dot_nt(jnp.concatenate([targets, parts], axis=1), sources) * scale_of(features) + norms
    return jnp.exp2(exponent).astype(BF16)


def flag_of(flags_ref, distance):
    columns = flags_ref.shape[1]
    lane = lax.broadcasted_iota(jnp.int32, (1, columns), 1)
    here = lane == distance + (columns - 1) // 2
    return jnp.sum(jnp.where(here, flags_ref[...], 0).astype(F32), axis=1, keepdims=True)


def flag_row(flags_ref):
    columns = flags_ref.shape[1]
    lane = lax.broadcasted_iota(jnp.int32, (1, LANES), 1)
    row = jnp.zeros((1, LANES), F32)
    for column in range(columns):
        row = jnp.where(lane == column, flag_of(flags_ref, column - (columns - 1) // 2), row)
    return row


def prepare_kernel(
    points_hbm, weights_hbm, interp_hbm, ci_hbm, rows_hbm, flags_hbm, ids_hbm,
    halo_ref, sv_ref, sum_ref, send_ref, flags_ref,
    points_ref, interp_ref, ci_ref, rows_ref, ids_ref, all_ref, arrived,
):
    features, points = points_ref.shape
    half, skeletons = points // 2, interp_ref.shape[1]
    pairs = (
        (rows_hbm, rows_ref),
        (points_hbm, points_ref),
        (weights_hbm, halo_ref.at[pl.ds(half, points)]),
        (interp_hbm, interp_ref),
        (ids_hbm, ids_ref),
        (ci_hbm, ci_ref),
        (flags_hbm, flags_ref),
    )
    copies = [pltpu.make_async_copy(source, place, arrived.at[i]) for i, (source, place) in enumerate(pairs)]
    for copy in copies:
        copy.start()
    leaf = lax.axis_index("leaf")
    core = leaf % 2
    cluster_count, picked = ids_ref.shape
    members = lax.axis_size("leaf") // cluster_count
    source_scale = -0.5 * scale_of(features)

    def packed(turned):
        n = turned.shape[1]
        return jnp.concatenate([turned[:, : n // 2], turned[:, n // 2 :]], axis=0).T

    def norms(turned):
        return source_scale * jnp.sum(turned * turned, axis=0, keepdims=True)

    copies[0].wait()
    one = (
        lax.broadcasted_iota(jnp.int32, (points, skeletons), 0) == rows_ref[...]
    ).astype(F32).astype(BF16)
    copies[1].wait()
    skeleton = dot_nn(points_ref[...], one)
    copies[2].wait()
    weights_turned = halo_ref[half : half + points, :].astype(F32).T.astype(BF16)
    copies[3].wait()
    charges_turned = dot_nn(weights_turned, interp_ref[...]).astype(BF16)
    copies[4].wait()
    ids = ids_ref[pl.ds(leaf // members, 1), :] - (leaf % members) * skeletons
    chosen = (
        lax.broadcasted_iota(jnp.int32, (skeletons, picked), 0) == ids
    ).astype(F32).astype(BF16)
    cluster = dot_nn(skeleton.astype(BF16), chosen)
    copies[5].wait()
    sums = dot_nn(charges_turned, ci_ref[...]).T
    part = picked // 2
    rows = sum_ref.shape[0]
    for h in range(2):
        columns = slice(h * part, (h + 1) * part)
        place = slice(h * rows, h * rows + part)
        all_ref[place, :] = sums[columns]
        place = slice(h * rows + part, h * rows + part + part // 2)
        all_ref[place, :] = packed(cluster[:, columns])
        place = slice(h * rows + part + part // 2, (h + 1) * rows)
        all_ref[place, :] = norm_block(norms(cluster[:, columns]))
    sum_ref[...] = all_ref[pl.ds(core * rows, rows), :]
    send_ref[...] = all_ref[pl.ds((1 - core) * rows, rows), :].astype(BF16)
    sk_half, sk_norms = skeletons // 2, norm_rows(skeletons)
    sv_ref[:sk_half, :] = packed(skeleton).astype(BF16)
    copies[6].wait()
    block = norm_block(norms(skeleton))
    row = lax.broadcasted_iota(jnp.int32, block.shape, 0)
    block = jnp.where(row == sk_norms - 1, flag_row(flags_ref), block)
    sv_ref[sk_half : sk_half + sk_norms, :] = block.astype(BF16)
    sv_ref[sk_half + sk_norms :, :] = charges_turned.astype(F32).T.astype(BF16)
    wide = points_ref[...].astype(F32)
    halo_ref[:half, :] = packed(wide).astype(BF16)
    halo_ref[half + points :, :] = norm_block(norms(wide)).astype(BF16)


def add_kernel(with_skeleton, last, sum_ref, got_ref, *refs):
    rows = sum_ref.shape[0]
    total = sum_ref[...] + got_ref[:rows, :].astype(F32)
    if with_skeleton:
        own_ref, other_ref, *refs = refs
        send_ref = refs[0]
        points = (send_ref.shape[0] - rows) // 2
        send_ref[rows : rows + points, :] = own_ref[:points, :]
        send_ref[rows + points :, :] = other_ref[:points, :]
    refs[0][:rows, :] = total.astype(BF16)
    if not last:
        refs[1][...] = total


def near_kernel(stage, across, features, *refs):
    leaf = lax.axis_index("leaf")
    core, chip = leaf % 2, (leaf // 2) % 2
    side, beside = 1 - 2 * core, 1 - 2 * chip
    first = stage == 0 and not across
    if first:
        flags_ref, halo_ref, low_ref, high_ref, parts_ref, near_ref, mass_ref = refs
        half = near_ref.shape[0] // 2
        forms = target_forms(halo_ref[:half, :], features)
        for ref, form in zip((low_ref, high_ref, parts_ref), forms):
            ref[...] = form
        distance = 0
    else:
        before_ref, flags_ref, halo_ref, low_ref, high_ref, parts_ref, near_ref, mass_ref = refs
        half = near_ref.shape[0] // 2
        if across:
            distance = side if stage == 0 else -side
        else:
            distance = 2 * beside if stage == 1 else -2 * beside

    def tile():
        flag = flag_of(flags_ref, distance)
        norms = source_norms(halo_ref[3 * half :, :], 2 * half)
        mass_ref[...] = (halo_ref[half : 3 * half, :].astype(F32) * flag).astype(BF16)
        step = min(SOURCE_ROWS, half)
        for start in range(0, 2 * half, TARGET_ROWS):
            rows = slice(start, min(start + TARGET_ROWS, 2 * half))
            total = None
            for place in range(0, half, step):
                sources = ones_beside(halo_ref[place : place + step, :])
                for h, ref in enumerate((low_ref, high_ref)):
                    terms = norms[h][:, place : place + step]
                    values = kernel_values(ref[rows, :], parts_ref[rows, :], sources, terms, features)
                    term = dot_nn(values, mass_ref[h * half + place : h * half + place + step, :])
                    total = term if total is None else total + term
            near_ref[rows, :] = total if first else before_ref[rows, :] + total

    if across and stage > 0:
        pl.when(core != chip if stage == 1 else core == chip)(tile)
    else:
        tile()


def grouped(count, rows):
    step = max(1, SOURCE_ROWS // rows)
    return [range(i, min(i + step, count)) for i in range(0, count, step)]


def sibling_kernel(masks, reduced, features, skeletons, reach, partner_ref, core_ref, *refs):
    pieces, (own_ref, other_ref, send_ref) = refs[: len(masks)], refs[len(masks) :]
    leaf = lax.axis_index("leaf")
    half, points = skeletons // 2, skeletons // 2 + norm_rows(skeletons)
    start = partner_ref.shape[0] - 2 * points
    blocks = [
        (0, pieces[0][:points, :]),
        (reduced, partner_ref[start : start + points, :]),
        (1, core_ref[:points, :]),
        (reduced | 1, partner_ref[start + points :, :]),
    ]
    forms = zip(*[target_forms(block[:half], features) for _, block in blocks])
    low, high, parts = [jnp.concatenate(form, axis=0) for form in forms]
    lane = lax.broadcasted_iota(jnp.int32, (1, LANES), 1)
    fields = [None] * len(blocks)
    for group in grouped(len(masks), half):
        sources = ones_beside(jnp.concatenate([pieces[i][:half, :] for i in group], axis=0))
        norms = [source_norms(pieces[i][half:points, :], skeletons) for i in group]
        mass = [pieces[i][points:, :].astype(F32) for i in group]
        masses = []
        for target, block in blocks:
            flags = block[points - 16 :].astype(F32)[15:16]
            kept = []
            for i in group:
                distance = (leaf ^ masks[i]) - (leaf ^ target)
                kept.append(1.0 - jnp.sum(jnp.where(lane == distance + reach, flags, 0.0), axis=1, keepdims=True))
            masses.append([(m * k).astype(BF16) for m, k in zip(mass, kept)])
        for h, targets in enumerate((low, high)):
            terms = jnp.concatenate([n[h] for n in norms], axis=1)
            values = kernel_values(targets, parts, sources, terms, features)
            for k in range(len(blocks)):
                both = jnp.concatenate([m[h * half : (h + 1) * half] for m in masses[k]], axis=0)
                term = dot_nn(values[k * skeletons : (k + 1) * skeletons], both)
                fields[k] = term if fields[k] is None else fields[k] + term
    own_ref[...] = fields[0]
    other_ref[...] = fields[1]
    send_ref[:skeletons, :] = fields[2].astype(BF16)
    send_ref[skeletons:, :] = fields[3].astype(BF16)


def field_kernel(own_ref, other_ref, got_ref, field_ref, send_ref):
    rows = own_ref.shape[0]
    field_ref[...] = own_ref[...] + got_ref[:rows, :].astype(F32)
    send_ref[...] = (other_ref[...] + got_ref[rows:, :].astype(F32)).astype(BF16)


def final_kernel(count, features, near_ref, interp_ref, sv_ref, own_ref, got_ref, *refs):
    packs, out_ref = refs[:count], refs[count]
    skeletons = interp_ref.shape[1]
    low, high, parts = target_forms(sv_ref[: skeletons // 2, :], features)
    half = max(r for r in range(1, packs[0].shape[0]) if 3 * r + norm_rows(2 * r) <= packs[0].shape[0])
    field = own_ref[...] + got_ref[...].astype(F32)
    for group in grouped(count, half):
        sources = ones_beside(jnp.concatenate([packs[i][2 * half : 3 * half, :] for i in group], axis=0))
        norms = [source_norms(packs[i][3 * half :, :], 2 * half) for i in group]
        for h, targets in enumerate((low, high)):
            terms = jnp.concatenate([n[h] for n in norms], axis=1)
            values = kernel_values(targets, parts, sources, terms, features)
            mass = jnp.concatenate([packs[i][h * half : (h + 1) * half, :] for i in group], axis=0)
            field += dot_nn(values, mass)
    coarse = field.astype(BF16)
    out_ref[...] = (near_ref[...] + dot_nn(interp_ref[...], coarse)).astype(out_ref.dtype)


def on_device(points, weights, interp, cluster_interp, skeleton_rows, near_flags, cluster_rows):
    leaves, groups = lax.axis_size("leaf"), lax.axis_size("group")
    leaf_points, features = points.shape
    columns = weights.shape[1]
    skeletons = interp.shape[1]
    cluster_count, picked = cluster_rows.shape
    members = leaves // cluster_count
    core_mask, chip_mask, reduced = 1, 2, 4
    half, part = leaf_points // 2, picked // 2
    sum_rows = part + part // 2 + norm_rows(part)
    sv_points = skeletons // 2 + norm_rows(skeletons)

    arguments = [points.T, weights, interp, cluster_interp, skeleton_rows, near_flags, cluster_rows]
    outs = [
        ((half + leaf_points + norm_rows(leaf_points), columns), BF16),
        ((sv_points + skeletons, columns), BF16),
        ((sum_rows, columns), F32),
        ((sum_rows, columns), BF16),
        (near_flags.shape, near_flags.dtype),
    ]
    scratch = [(x.shape, x.dtype) for x in (arguments[0], interp, cluster_interp, skeleton_rows, cluster_rows)]
    scratch += [((2 * sum_rows, columns), F32)]
    halo, skeleton, cluster_sum, cluster_send, flags = pl.pallas_call(
        prepare_kernel,
        out_shape=[jax.ShapeDtypeStruct(shape, dtype) for shape, dtype in outs],
        in_specs=[pl.BlockSpec(memory_space=pltpu.HBM) for _ in arguments],
        out_specs=[vmem() for _ in outs],
        scratch_shapes=[pltpu.VMEM(shape, dtype) for shape, dtype in scratch]
        + [pltpu.SemaphoreType.DMA((len(arguments),))],
        compiler_params=pltpu.CompilerParams(vmem_limit_bytes=VMEM_BYTES),
        cost_estimate=pl.CostEstimate(flops=10**6, bytes_accessed=0, transcendentals=0),
    )(*[pltpu.with_memory_space_constraint(x, pltpu.HBM) for x in arguments])

    have, done = {}, {}
    add_masks = [1 << i for i in reversed(range(1, members.bit_length() - 1))]
    adds = dict(zip(("first_add", "add_a", "add_b", "add_c"), add_masks + [0]))
    gather_masks = [1 << i for i in reversed(range(2, leaves.bit_length() - 1)) if 1 << i != reduced]
    piece_masks = [m for m in range(leaves) if not m & (reduced | core_mask)]
    reach = (near_flags.shape[1] - 1) // 2
    ahead = [(i, i + 4) for i in range(leaves - 4) if i & chip_mask == 0]
    behind = [(i, i - 4) for i in range(4, leaves) if i & chip_mask != 0]
    tile = ((leaf_points, columns), BF16)
    near_ins = {
        "near_core": (0, True, "halo_core"),
        "near_beside": (1, False, "halo_beside"),
        "near_across": (1, True, "halo_across"),
        "near_far": (2, False, "halo_far"),
        "near_last": (2, True, "halo_last"),
    }

    def get(name):
        if name not in have:
            value = arrive(name)
            if name in RELEASES:
                value = hand_on(value, done[RELEASES[name]])
            have[name] = value
        return have[name]

    def arrive(name):
        if name == "sv_1":
            return xor_exchange(skeleton, "leaf", core_mask)
        if name.startswith("sv_"):
            mask = int(name[3:])
            if mask == 0:
                return skeleton
            step = core_mask if mask & core_mask else chip_mask if mask & chip_mask else mask & -mask
            return xor_exchange(get(f"sv_{mask ^ step}"), "leaf", step)
        if name == "halo_core":
            return xor_exchange(halo, "leaf", core_mask)
        if name == "halo_beside":
            return xor_exchange(halo, "leaf", chip_mask)
        if name == "halo_next":
            return get("halo_beside")
        if name == "halo_across":
            return xor_exchange(get("halo_next"), "leaf", core_mask)
        if name == "halo_far":
            return lax.ppermute(get("halo_next"), "leaf", ahead + behind)
        if name == "halo_last":
            return xor_exchange(get("halo_far"), "leaf", core_mask)
        if name == "field":
            return xor_exchange(have["field_send"], "leaf", reduced)
        if name.startswith("sum_"):
            return xor_exchange(have["sum_send"], "leaf", int(name[4:]))
        if name == "packs":
            own_group = [have["sum_send"]]
            mask = members
            while mask < leaves:
                own_group += [xor_exchange(pack, "leaf", mask) for pack in own_group]
                mask *= 2
            packs = []
            for shift in range(1, groups):
                order = [(i, (i + shift) % groups) for i in range(groups)]
                packs += [lax.ppermute(pack, "group", order) for pack in own_group]
            return jnp.concatenate(packs, axis=0) if len(packs) > 1 else packs[0]
        if name == "packs_core":
            return xor_exchange(get("packs"), "leaf", core_mask)
        raise KeyError(name)

    have["sum"], have["sum_send"] = cluster_sum, cluster_send
    have["sum_1"] = xor_exchange(cluster_send, "leaf", core_mask)
    received, token = "sum_1", None
    for name, work in ORDER.items():
        after = ([token] if token is not None else []) + [get(x) for x in DEADLINES.get(name, ())]
        if name in adds:
            mask, last = adds[name], adds[name] == 0
            with_skeleton = mask == reduced
            rows = sum_rows + (2 * sv_points if with_skeleton else 0)
            outs = [((rows, columns), BF16)] + ([] if last else [((sum_rows, columns), F32)])
            ins = [have["sum"], have[received]] + ([get("sv_0"), get("sv_1")] if with_skeleton else [])
            body = functools.partial(add_kernel, with_skeleton, last)
            have["sum_send"], *total = call(body, outs, ins, after=after, work=work)
            token = have["sum_send"]
            if not last:
                have["sum"], received = total[0], f"sum_{mask}"
                have[received] = arrive(received)
            else:
                get("packs")
        elif name == "near_self":
            *targets, near = call(
                functools.partial(near_kernel, 0, False, features),
                [tile, tile, tile, ((leaf_points, columns), F32)],
                [flags, halo],
                scratch=[((leaf_points, columns), BF16)],
                after=after,
                work=work,
            )
            token = near
        elif name in near_ins:
            stage, across, source = near_ins[name]
            (near,) = call(
                functools.partial(near_kernel, stage, across, features),
                [((leaf_points, columns), F32)],
                [near, flags, get(source), *targets],
                scratch=[((leaf_points, columns), BF16)],
                after=after if token is not near else after[1:],
                in_place=True,
                work=work,
            )
            token = near
        elif name == "sibling":
            *fields, have["field_send"] = call(
                functools.partial(sibling_kernel, piece_masks, reduced, features, skeletons, reach),
                [((skeletons, columns), F32)] * 2 + [((2 * skeletons, columns), BF16)],
                [have[f"sum_{reduced}"], get("sv_1")] + [get(f"sv_{m}") for m in piece_masks],
                after=after,
                work=work,
            )
            token = fields[0]
            have["field_core"] = xor_exchange(have["field_send"], "leaf", core_mask)
        elif name == "field":
            field, have["field_send"] = call(
                field_kernel,
                [((skeletons, columns), F32), ((skeletons, columns), BF16)],
                fields + [have["field_core"]],
                after=after,
                work=work,
            )
            token = field
            get("field")
        elif name == "final":
            packs = [get("packs"), get("packs_core")]
            packs = [p[i : i + sum_rows] for p in packs for i in range(0, p.shape[0], sum_rows)]
            (token,) = call(
                functools.partial(final_kernel, len(packs), features),
                [((leaf_points, columns), BF16)],
                [near, interp, get("sv_0"), field, get("field")] + packs,
                work=work,
            )
        done[name] = token
    return token


def solution(mesh):
    placed = (P(("group", "leaf"), None),) * 6 + (P("group", None),)
    return jax.shard_map(
        on_device, mesh=mesh, in_specs=placed, out_specs=P(("group", "leaf"), None), check_vma=False
    )
```

```python
import functools
import math

import jax
import jax.numpy as jnp
from jax import lax
from jax.experimental import pallas as pl
from jax.experimental.pallas import tpu as pltpu
from jax.sharding import PartitionSpec as P

BF16 = jnp.bfloat16
F32 = jnp.float32
VMEM_BYTES = 24 * 1024 * 1024
LANES = 128
TARGET_ROWS = 512
SOURCE_ROWS = 512
ORDER = {
    "first_add": 1000000,
    "near_self": 2000000000,
    "near_core": 2000000000,
    "near_beside": 2000000000,
    "add_a": 1000000,
    "add_b": 1000000,
    "sibling": 2000000000,
    "near_across": 2000000000,
    "add_c": 1000000,
    "field": 1000000,
    "near_far": 2000000000,
    "near_last": 2000000000,
    "final": 2000000000,
}
DEADLINES = {
    "add_a": ["sv_8"],
    "sibling": ["sv_10"],
    "field": ["packs"],
}
RELEASES = {"sv_0": "first_add", "halo_next": "near_core", "halo_far": "field"}


def vmem():
    return pl.BlockSpec(memory_space=pltpu.VMEM)


def call(body, outs, ins, scratch=(), after=(), in_place=False, work=10**6):
    waits = len(after)
    return pl.pallas_call(
        lambda *refs: body(*refs[waits:]),
        out_shape=[jax.ShapeDtypeStruct(shape, dtype) for shape, dtype in outs],
        in_specs=[pl.BlockSpec(memory_space=pl.ANY) for _ in after] + [vmem() for _ in ins],
        out_specs=[vmem() for _ in outs],
        scratch_shapes=[pltpu.VMEM(shape, dtype) for shape, dtype in scratch],
        input_output_aliases={waits: 0} if in_place else {},
        compiler_params=pltpu.CompilerParams(vmem_limit_bytes=VMEM_BYTES),
        cost_estimate=pl.CostEstimate(flops=work, bytes_accessed=0, transcendentals=0),
    )(*after, *ins)


def hand_on(value, *after):
    return pl.pallas_call(
        lambda *refs: None,
        out_shape=jax.ShapeDtypeStruct(value.shape, value.dtype),
        in_specs=[vmem()] + [pl.BlockSpec(memory_space=pl.ANY) for _ in after],
        out_specs=vmem(),
        input_output_aliases={0: 0},
        compiler_params=pltpu.CompilerParams(vmem_limit_bytes=VMEM_BYTES),
        cost_estimate=pl.CostEstimate(flops=0, bytes_accessed=0, transcendentals=0),
    )(value, *after)


def dot_nt(a, b):
    return lax.dot_general(a, b, (((1,), (1,)), ((), ())), preferred_element_type=F32)


def dot_nn(a, b):
    return jnp.dot(a, b, preferred_element_type=F32)


def xor_exchange(value, axis, mask):
    return lax.ppermute(value, axis, [(i, i ^ mask) for i in range(lax.axis_size(axis))])


def up16(rows):
    return -(-rows // 16) * 16


def norm_rows(points):
    return up16(3 * points // LANES)


def scale_of(features):
    return 4.0 / features * math.log2(math.e)


def three_parts(values):
    high = values.astype(BF16).astype(F32)
    rest = values - high
    middle = rest.astype(BF16).astype(F32)
    return high, middle, rest - middle


def norm_block(norms):
    count = norms.shape[1] // LANES
    parts = [
        part[:, i * LANES : (i + 1) * LANES] for part in three_parts(norms) for i in range(count)
    ]
    rest = norm_rows(norms.shape[1]) - len(parts)
    return jnp.concatenate(parts + [jnp.zeros((rest, LANES), F32)], axis=0)


def source_norms(block, points):
    count = points // LANES
    block = block.astype(F32)
    rows = block[:count] + block[count : 2 * count] + block[2 * count : 3 * count]
    return tuple(
        jnp.concatenate([rows[i : i + 1] for i in range(h * count // 2, (h + 1) * count // 2)], axis=1)
        for h in range(2)
    )


def target_forms(packed, features):
    wide = packed.astype(F32)
    turned = pltpu.roll(wide, features, 1)
    lane = lax.broadcasted_iota(jnp.int32, wide.shape, 1)
    low, high, norms = [], [], []
    for first, second in ((wide, turned), (turned, wide)):
        kept = jnp.where(lane < features, first, 0.0)
        low.append(kept)
        high.append(jnp.where(lane >= features, second, 0.0))
        parts = three_parts(-0.5 * jnp.sum(kept * kept, axis=1, keepdims=True))
        norms.append(
            jnp.where(lane == 0, parts[0], jnp.where(lane == 1, parts[1], jnp.where(lane == 2, parts[2], 0.0)))
        )
    return tuple(jnp.concatenate(form, axis=0).astype(BF16) for form in (low, high, norms))


def ones_beside(packed):
    lane = lax.broadcasted_iota(jnp.int32, packed.shape, 1)
    return jnp.concatenate([packed, jnp.where(lane < 3, 1.0, 0.0).astype(BF16)], axis=1)


def kernel_values(targets, parts, sources, norms, features):
    exponent = dot_nt(jnp.concatenate([targets, parts], axis=1), sources) * scale_of(features) + norms
    return jnp.exp2(exponent).astype(BF16)


def flag_of(flags_ref, distance):
    columns = flags_ref.shape[1]
    lane = lax.broadcasted_iota(jnp.int32, (1, columns), 1)
    here = lane == distance + (columns - 1) // 2
    return jnp.sum(jnp.where(here, flags_ref[...], 0).astype(F32), axis=1, keepdims=True)


def flag_row(flags_ref):
    columns = flags_ref.shape[1]
    lane = lax.broadcasted_iota(jnp.int32, (1, LANES), 1)
    row = jnp.zeros((1, LANES), F32)
    for column in range(columns):
        row = jnp.where(lane == column, flag_of(flags_ref, column - (columns - 1) // 2), row)
    return row


def prepare_kernel(
    points_hbm, weights_hbm, interp_hbm, ci_hbm, rows_hbm, flags_hbm, ids_hbm,
    halo_ref, sv_ref, sum_ref, send_ref, flags_ref,
    points_ref, interp_ref, ci_ref, rows_ref, ids_ref, all_ref, arrived,
):
    features, points = points_ref.shape
    half, skeletons = points // 2, interp_ref.shape[1]
    pairs = (
        (rows_hbm, rows_ref),
        (points_hbm, points_ref),
        (weights_hbm, halo_ref.at[pl.ds(half, points)]),
        (interp_hbm, interp_ref),
        (ids_hbm, ids_ref),
        (ci_hbm, ci_ref),
        (flags_hbm, flags_ref),
    )
    copies = [pltpu.make_async_copy(source, place, arrived.at[i]) for i, (source, place) in enumerate(pairs)]
    for copy in copies:
        copy.start()
    leaf = lax.axis_index("leaf")
    core = leaf % 2
    cluster_count, picked = ids_ref.shape
    members = lax.axis_size("leaf") // cluster_count
    source_scale = -0.5 * scale_of(features)

    def packed(turned):
        n = turned.shape[1]
        return jnp.concatenate([turned[:, : n // 2], turned[:, n // 2 :]], axis=0).T

    def norms(turned):
        return source_scale * jnp.sum(turned * turned, axis=0, keepdims=True)

    copies[0].wait()
    one = (
        lax.broadcasted_iota(jnp.int32, (points, skeletons), 0) == rows_ref[...]
    ).astype(F32).astype(BF16)
    copies[1].wait()
    skeleton = dot_nn(points_ref[...], one)
    copies[2].wait()
    weights_turned = halo_ref[half : half + points, :].astype(F32).T.astype(BF16)
    copies[3].wait()
    charges_turned = dot_nn(weights_turned, interp_ref[...]).astype(BF16)
    copies[4].wait()
    ids = ids_ref[pl.ds(leaf // members, 1), :] - (leaf % members) * skeletons
    chosen = (
        lax.broadcasted_iota(jnp.int32, (skeletons, picked), 0) == ids
    ).astype(F32).astype(BF16)
    cluster = dot_nn(skeleton.astype(BF16), chosen)
    copies[5].wait()
    sums = dot_nn(charges_turned, ci_ref[...]).T
    part = picked // 2
    rows = sum_ref.shape[0]
    for h in range(2):
        columns = slice(h * part, (h + 1) * part)
        place = slice(h * rows, h * rows + part)
        all_ref[place, :] = sums[columns]
        place = slice(h * rows + part, h * rows + part + part // 2)
        all_ref[place, :] = packed(cluster[:, columns])
        place = slice(h * rows + part + part // 2, (h + 1) * rows)
        all_ref[place, :] = norm_block(norms(cluster[:, columns]))
    sum_ref[...] = all_ref[pl.ds(core * rows, rows), :]
    send_ref[...] = all_ref[pl.ds((1 - core) * rows, rows), :].astype(BF16)
    sk_half, sk_norms = skeletons // 2, norm_rows(skeletons)
    sv_ref[:sk_half, :] = packed(skeleton).astype(BF16)
    copies[6].wait()
    block = norm_block(norms(skeleton))
    row = lax.broadcasted_iota(jnp.int32, block.shape, 0)
    block = jnp.where(row == sk_norms - 1, flag_row(flags_ref), block)
    sv_ref[sk_half : sk_half + sk_norms, :] = block.astype(BF16)
    sv_ref[sk_half + sk_norms :, :] = charges_turned.astype(F32).T.astype(BF16)
    wide = points_ref[...].astype(F32)
    halo_ref[:half, :] = packed(wide).astype(BF16)
    halo_ref[half + points :, :] = norm_block(norms(wide)).astype(BF16)


def add_kernel(with_skeleton, last, sum_ref, got_ref, *refs):
    rows = sum_ref.shape[0]
    total = sum_ref[...] + got_ref[:rows, :].astype(F32)
    if with_skeleton:
        own_ref, other_ref, *refs = refs
        send_ref = refs[0]
        points = (send_ref.shape[0] - rows) // 2
        send_ref[rows : rows + points, :] = own_ref[:points, :]
        send_ref[rows + points :, :] = other_ref[:points, :]
    refs[0][:rows, :] = total.astype(BF16)
    if not last:
        refs[1][...] = total


def near_kernel(stage, across, features, *refs):
    leaf = lax.axis_index("leaf")
    core, chip = leaf % 2, (leaf // 2) % 2
    side, beside = 1 - 2 * core, 1 - 2 * chip
    first = stage == 0 and not across
    if first:
        flags_ref, halo_ref, low_ref, high_ref, parts_ref, near_ref, mass_ref = refs
        half = near_ref.shape[0] // 2
        forms = target_forms(halo_ref[:half, :], features)
        for ref, form in zip((low_ref, high_ref, parts_ref), forms):
            ref[...] = form
        distance = 0
    else:
        before_ref, flags_ref, halo_ref, low_ref, high_ref, parts_ref, near_ref, mass_ref = refs
        half = near_ref.shape[0] // 2
        if across:
            distance = side if stage == 0 else -side
        else:
            distance = 2 * beside if stage == 1 else -2 * beside

    def tile():
        flag = flag_of(flags_ref, distance)
        norms = source_norms(halo_ref[3 * half :, :], 2 * half)
        mass_ref[...] = (halo_ref[half : 3 * half, :].astype(F32) * flag).astype(BF16)
        step = min(SOURCE_ROWS, half)
        for start in range(0, 2 * half, TARGET_ROWS):
            rows = slice(start, min(start + TARGET_ROWS, 2 * half))
            total = None
            for place in range(0, half, step):
                sources = ones_beside(halo_ref[place : place + step, :])
                for h, ref in enumerate((low_ref, high_ref)):
                    terms = norms[h][:, place : place + step]
                    values = kernel_values(ref[rows, :], parts_ref[rows, :], sources, terms, features)
                    term = dot_nn(values, mass_ref[h * half + place : h * half + place + step, :])
                    total = term if total is None else total + term
            near_ref[rows, :] = total if first else before_ref[rows, :] + total

    if across and stage > 0:
        pl.when(core != chip if stage == 1 else core == chip)(tile)
    else:
        tile()


def grouped(count, rows):
    step = max(1, SOURCE_ROWS // rows)
    return [range(i, min(i + step, count)) for i in range(0, count, step)]


def sibling_kernel(masks, reduced, features, skeletons, reach, partner_ref, core_ref, *refs):
    pieces, (own_ref, other_ref, send_ref) = refs[: len(masks)], refs[len(masks) :]
    leaf = lax.axis_index("leaf")
    half, points = skeletons // 2, skeletons // 2 + norm_rows(skeletons)
    start = partner_ref.shape[0] - 2 * points
    blocks = [
        (0, pieces[0][:points, :]),
        (reduced, partner_ref[start : start + points, :]),
        (1, core_ref[:points, :]),
        (reduced | 1, partner_ref[start + points :, :]),
    ]
    forms = zip(*[target_forms(block[:half], features) for _, block in blocks])
    low, high, parts = [jnp.concatenate(form, axis=0) for form in forms]
    lane = lax.broadcasted_iota(jnp.int32, (1, LANES), 1)
    fields = [None] * len(blocks)
    for group in grouped(len(masks), half):
        sources = ones_beside(jnp.concatenate([pieces[i][:half, :] for i in group], axis=0))
        norms = [source_norms(pieces[i][half:points, :], skeletons) for i in group]
        mass = [pieces[i][points:, :].astype(F32) for i in group]
        masses = []
        for target, block in blocks:
            flags = block[points - 16 :].astype(F32)[15:16]
            kept = []
            for i in group:
                distance = (leaf ^ masks[i]) - (leaf ^ target)
                kept.append(1.0 - jnp.sum(jnp.where(lane == distance + reach, flags, 0.0), axis=1, keepdims=True))
            masses.append([(m * k).astype(BF16) for m, k in zip(mass, kept)])
        for h, targets in enumerate((low, high)):
            terms = jnp.concatenate([n[h] for n in norms], axis=1)
            values = kernel_values(targets, parts, sources, terms, features)
            for k in range(len(blocks)):
                both = jnp.concatenate([m[h * half : (h + 1) * half] for m in masses[k]], axis=0)
                term = dot_nn(values[k * skeletons : (k + 1) * skeletons], both)
                fields[k] = term if fields[k] is None else fields[k] + term
    own_ref[...] = fields[0]
    other_ref[...] = fields[1]
    send_ref[:skeletons, :] = fields[2].astype(BF16)
    send_ref[skeletons:, :] = fields[3].astype(BF16)


def field_kernel(own_ref, other_ref, got_ref, field_ref, send_ref):
    rows = own_ref.shape[0]
    field_ref[...] = own_ref[...] + got_ref[:rows, :].astype(F32)
    send_ref[...] = (other_ref[...] + got_ref[rows:, :].astype(F32)).astype(BF16)


def final_kernel(count, features, near_ref, interp_ref, sv_ref, own_ref, got_ref, *refs):
    packs, out_ref = refs[:count], refs[count]
    skeletons = interp_ref.shape[1]
    low, high, parts = target_forms(sv_ref[: skeletons // 2, :], features)
    half = max(r for r in range(1, packs[0].shape[0]) if 3 * r + norm_rows(2 * r) <= packs[0].shape[0])
    field = own_ref[...] + got_ref[...].astype(F32)
    for group in grouped(count, half):
        sources = ones_beside(jnp.concatenate([packs[i][2 * half : 3 * half, :] for i in group], axis=0))
        norms = [source_norms(packs[i][3 * half :, :], 2 * half) for i in group]
        for h, targets in enumerate((low, high)):
            terms = jnp.concatenate([n[h] for n in norms], axis=1)
            values = kernel_values(targets, parts, sources, terms, features)
            mass = jnp.concatenate([packs[i][h * half : (h + 1) * half, :] for i in group], axis=0)
            field += dot_nn(values, mass)
    coarse = field.astype(BF16)
    out_ref[...] = (near_ref[...] + dot_nn(interp_ref[...], coarse)).astype(out_ref.dtype)


def on_device(points, weights, interp, cluster_interp, skeleton_rows, near_flags, cluster_rows):
    leaves, groups = lax.axis_size("leaf"), lax.axis_size("group")
    leaf_points, features = points.shape
    columns = weights.shape[1]
    skeletons = interp.shape[1]
    cluster_count, picked = cluster_rows.shape
    members = leaves // cluster_count
    core_mask, chip_mask, reduced = 1, 2, 4
    half, part = leaf_points // 2, picked // 2
    sum_rows = part + part // 2 + norm_rows(part)
    sv_points = skeletons // 2 + norm_rows(skeletons)

    arguments = [points.T, weights, interp, cluster_interp, skeleton_rows, near_flags, cluster_rows]
    outs = [
        ((half + leaf_points + norm_rows(leaf_points), columns), BF16),
        ((sv_points + skeletons, columns), BF16),
        ((sum_rows, columns), F32),
        ((sum_rows, columns), BF16),
        (near_flags.shape, near_flags.dtype),
    ]
    scratch = [(x.shape, x.dtype) for x in (arguments[0], interp, cluster_interp, skeleton_rows, cluster_rows)]
    scratch += [((2 * sum_rows, columns), F32)]
    halo, skeleton, cluster_sum, cluster_send, flags = pl.pallas_call(
        prepare_kernel,
        out_shape=[jax.ShapeDtypeStruct(shape, dtype) for shape, dtype in outs],
        in_specs=[pl.BlockSpec(memory_space=pltpu.HBM) for _ in arguments],
        out_specs=[vmem() for _ in outs],
        scratch_shapes=[pltpu.VMEM(shape, dtype) for shape, dtype in scratch]
        + [pltpu.SemaphoreType.DMA((len(arguments),))],
        compiler_params=pltpu.CompilerParams(vmem_limit_bytes=VMEM_BYTES),
        cost_estimate=pl.CostEstimate(flops=10**6, bytes_accessed=0, transcendentals=0),
    )(*[pltpu.with_memory_space_constraint(x, pltpu.HBM) for x in arguments])

    have, done = {}, {}
    add_masks = [1 << i for i in reversed(range(1, members.bit_length() - 1))]
    adds = dict(zip(("first_add", "add_a", "add_b", "add_c"), add_masks + [0]))
    gather_masks = [1 << i for i in reversed(range(2, leaves.bit_length() - 1)) if 1 << i != reduced]
    piece_masks = [m for m in range(leaves) if not m & (reduced | core_mask)]
    reach = (near_flags.shape[1] - 1) // 2
    ahead = [(i, i + 4) for i in range(leaves - 4) if i & chip_mask == 0]
    behind = [(i, i - 4) for i in range(4, leaves) if i & chip_mask != 0]
    tile = ((leaf_points, columns), BF16)
    near_ins = {
        "near_core": (0, True, "halo_core"),
        "near_beside": (1, False, "halo_next"),
        "near_across": (1, True, "halo_across"),
        "near_far": (2, False, "halo_far"),
        "near_last": (2, True, "halo_last"),
    }

    def get(name):
        if name not in have:
            value = arrive(name)
            if name in RELEASES:
                value = hand_on(value, done[RELEASES[name]])
            have[name] = value
        return have[name]

    def arrive(name):
        if name == "sv_1":
            return xor_exchange(skeleton, "leaf", core_mask)
        if name.startswith("sv_"):
            mask = int(name[3:])
            if mask == 0:
                return skeleton
            step = core_mask if mask & core_mask else chip_mask if mask & chip_mask else mask & -mask
            return xor_exchange(get(f"sv_{mask ^ step}"), "leaf", step)
        if name == "halo_core":
            return xor_exchange(halo, "leaf", core_mask)
        if name == "halo_beside":
            return xor_exchange(halo, "leaf", chip_mask)
        if name == "halo_next":
            return get("halo_beside")
        if name == "halo_across":
            return xor_exchange(get("halo_next"), "leaf", core_mask)
        if name == "halo_far":
            return lax.ppermute(get("halo_next"), "leaf", ahead + behind)
        if name == "halo_last":
            return xor_exchange(get("halo_far"), "leaf", core_mask)
        if name == "field":
            return xor_exchange(have["field_send"], "leaf", reduced)
        if name.startswith("sum_"):
            return xor_exchange(have["sum_send"], "leaf", int(name[4:]))
        if name == "packs":
            own_group = [have["sum_send"]]
            mask = members
            while mask < leaves:
                own_group += [xor_exchange(pack, "leaf", mask) for pack in own_group]
                mask *= 2
            packs = []
            for shift in range(1, groups):
                order = [(i, (i + shift) % groups) for i in range(groups)]
                packs += [lax.ppermute(pack, "group", order) for pack in own_group]
            return jnp.concatenate(packs, axis=0) if len(packs) > 1 else packs[0]
        if name == "packs_core":
            return xor_exchange(get("packs"), "leaf", core_mask)
        raise KeyError(name)

    have["sum"], have["sum_send"] = cluster_sum, cluster_send
    have["sum_1"] = xor_exchange(cluster_send, "leaf", core_mask)
    received, token = "sum_1", None
    for name, work in ORDER.items():
        after = ([token] if token is not None else []) + [get(x) for x in DEADLINES.get(name, ())]
        if name in adds:
            mask, last = adds[name], adds[name] == 0
            with_skeleton = mask == reduced
            rows = sum_rows + (2 * sv_points if with_skeleton else 0)
            outs = [((rows, columns), BF16)] + ([] if last else [((sum_rows, columns), F32)])
            ins = [have["sum"], have[received]] + ([get("sv_0"), get("sv_1")] if with_skeleton else [])
            body = functools.partial(add_kernel, with_skeleton, last)
            have["sum_send"], *total = call(body, outs, ins, after=after, work=work)
            token = have["sum_send"]
            if not last:
                have["sum"], received = total[0], f"sum_{mask}"
                have[received] = arrive(received)
            else:
                get("packs")
        elif name == "near_self":
            *targets, near = call(
                functools.partial(near_kernel, 0, False, features),
                [tile, tile, tile, ((leaf_points, columns), F32)],
                [flags, halo],
                scratch=[((leaf_points, columns), BF16)],
                after=after,
                work=work,
            )
            token = near
        elif name in near_ins:
            stage, across, source = near_ins[name]
            (near,) = call(
                functools.partial(near_kernel, stage, across, features),
                [((leaf_points, columns), F32)],
                [near, flags, get(source), *targets],
                scratch=[((leaf_points, columns), BF16)],
                after=after if token is not near else after[1:],
                in_place=True,
                work=work,
            )
            token = near
        elif name == "sibling":
            *fields, have["field_send"] = call(
                functools.partial(sibling_kernel, piece_masks, reduced, features, skeletons, reach),
                [((skeletons, columns), F32)] * 2 + [((2 * skeletons, columns), BF16)],
                [have[f"sum_{reduced}"], get("sv_1")] + [get(f"sv_{m}") for m in piece_masks],
                after=after,
                work=work,
            )
            token = fields[0]
            have["field_core"] = xor_exchange(have["field_send"], "leaf", core_mask)
        elif name == "field":
            field, have["field_send"] = call(
                field_kernel,
                [((skeletons, columns), F32), ((skeletons, columns), BF16)],
                fields + [have["field_core"]],
                after=after,
                work=work,
            )
            token = field
            get("field")
        elif name == "final":
            packs = [get("packs"), get("packs_core")]
            packs = [p[i : i + sum_rows] for p in packs for i in range(0, p.shape[0], sum_rows)]
            (token,) = call(
                functools.partial(final_kernel, len(packs), features),
                [((leaf_points, columns), BF16)],
                [near, interp, get("sv_0"), field, get("field")] + packs,
                work=work,
            )
        done[name] = token
    return token


def solution(mesh):
    placed = (P(("group", "leaf"), None),) * 6 + (P("group", None),)
    return jax.shard_map(
        on_device, mesh=mesh, in_specs=placed, out_specs=P(("group", "leaf"), None), check_vma=False
    )
```

```python
import functools
import math

import jax
import jax.numpy as jnp
from jax import lax
from jax.experimental import pallas as pl
from jax.experimental.pallas import tpu as pltpu
from jax.sharding import PartitionSpec as P

BF16 = jnp.bfloat16
F32 = jnp.float32
VMEM_BYTES = 24 * 1024 * 1024
LANES = 128
TARGET_ROWS = 512
SOURCE_ROWS = 512
ORDER = {
    "first_add": 1000000,
    "near_self": 2000000000,
    "near_core": 2000000000,
    "near_beside": 300000000,
    "add_a": 1000000,
    "add_b": 1000000,
    "sibling": 2000000000,
    "near_across": 2000000000,
    "add_c": 1000000,
    "field": 1000000,
    "near_far": 2000000000,
    "near_last": 2000000000,
    "final": 2000000000,
}
DEADLINES = {
    "add_a": ["sv_8"],
    "sibling": ["sv_10"],
}
RELEASES = {"sv_0": ["first_add"], "halo_next": ["near_core"], "halo_far": ["field", "packs"]}


def vmem():
    return pl.BlockSpec(memory_space=pltpu.VMEM)


def call(body, outs, ins, scratch=(), after=(), in_place=False, work=10**6):
    waits = len(after)
    return pl.pallas_call(
        lambda *refs: body(*refs[waits:]),
        out_shape=[jax.ShapeDtypeStruct(shape, dtype) for shape, dtype in outs],
        in_specs=[pl.BlockSpec(memory_space=pl.ANY) for _ in after] + [vmem() for _ in ins],
        out_specs=[vmem() for _ in outs],
        scratch_shapes=[pltpu.VMEM(shape, dtype) for shape, dtype in scratch],
        input_output_aliases={waits: 0} if in_place else {},
        compiler_params=pltpu.CompilerParams(vmem_limit_bytes=VMEM_BYTES),
        cost_estimate=pl.CostEstimate(flops=work, bytes_accessed=0, transcendentals=0),
    )(*after, *ins)


def hand_on(value, *after):
    return pl.pallas_call(
        lambda *refs: None,
        out_shape=jax.ShapeDtypeStruct(value.shape, value.dtype),
        in_specs=[vmem()] + [pl.BlockSpec(memory_space=pl.ANY) for _ in after],
        out_specs=vmem(),
        input_output_aliases={0: 0},
        compiler_params=pltpu.CompilerParams(vmem_limit_bytes=VMEM_BYTES),
        cost_estimate=pl.CostEstimate(flops=0, bytes_accessed=0, transcendentals=0),
    )(value, *after)


def dot_nt(a, b):
    return lax.dot_general(a, b, (((1,), (1,)), ((), ())), preferred_element_type=F32)


def dot_nn(a, b):
    return jnp.dot(a, b, preferred_element_type=F32)


def xor_exchange(value, axis, mask):
    return lax.ppermute(value, axis, [(i, i ^ mask) for i in range(lax.axis_size(axis))])


def up16(rows):
    return -(-rows // 16) * 16


def norm_rows(points):
    return up16(3 * points // LANES)


def scale_of(features):
    return 4.0 / features * math.log2(math.e)


def three_parts(values):
    high = values.astype(BF16).astype(F32)
    rest = values - high
    middle = rest.astype(BF16).astype(F32)
    return high, middle, rest - middle


def norm_block(norms):
    count = norms.shape[1] // LANES
    parts = [
        part[:, i * LANES : (i + 1) * LANES] for part in three_parts(norms) for i in range(count)
    ]
    rest = norm_rows(norms.shape[1]) - len(parts)
    return jnp.concatenate(parts + [jnp.zeros((rest, LANES), F32)], axis=0)


def source_norms(block, points):
    count = points // LANES
    block = block.astype(F32)
    rows = block[:count] + block[count : 2 * count] + block[2 * count : 3 * count]
    return tuple(
        jnp.concatenate([rows[i : i + 1] for i in range(h * count // 2, (h + 1) * count // 2)], axis=1)
        for h in range(2)
    )


def target_forms(packed, features):
    wide = packed.astype(F32)
    turned = pltpu.roll(wide, features, 1)
    lane = lax.broadcasted_iota(jnp.int32, wide.shape, 1)
    low, high, norms = [], [], []
    for first, second in ((wide, turned), (turned, wide)):
        kept = jnp.where(lane < features, first, 0.0)
        low.append(kept)
        high.append(jnp.where(lane >= features, second, 0.0))
        parts = three_parts(-0.5 * jnp.sum(kept * kept, axis=1, keepdims=True))
        norms.append(
            jnp.where(lane == 0, parts[0], jnp.where(lane == 1, parts[1], jnp.where(lane == 2, parts[2], 0.0)))
        )
    return tuple(jnp.concatenate(form, axis=0).astype(BF16) for form in (low, high, norms))


def ones_beside(packed):
    lane = lax.broadcasted_iota(jnp.int32, packed.shape, 1)
    return jnp.concatenate([packed, jnp.where(lane < 3, 1.0, 0.0).astype(BF16)], axis=1)


def kernel_values(targets, parts, sources, norms, features):
    exponent = dot_nt(jnp.concatenate([targets, parts], axis=1), sources) * scale_of(features) + norms
    return jnp.exp2(exponent).astype(BF16)


def flag_of(flags_ref, distance):
    columns = flags_ref.shape[1]
    lane = lax.broadcasted_iota(jnp.int32, (1, columns), 1)
    here = lane == distance + (columns - 1) // 2
    return jnp.sum(jnp.where(here, flags_ref[...], 0).astype(F32), axis=1, keepdims=True)


def flag_row(flags_ref):
    columns = flags_ref.shape[1]
    lane = lax.broadcasted_iota(jnp.int32, (1, LANES), 1)
    row = jnp.zeros((1, LANES), F32)
    for column in range(columns):
        row = jnp.where(lane == column, flag_of(flags_ref, column - (columns - 1) // 2), row)
    return row


def prepare_kernel(
    points_hbm, weights_hbm, interp_hbm, ci_hbm, rows_hbm, flags_hbm, ids_hbm,
    halo_ref, sv_ref, sum_ref, send_ref, flags_ref,
    points_ref, interp_ref, ci_ref, rows_ref, ids_ref, all_ref, arrived,
):
    features, points = points_ref.shape
    half, skeletons = points // 2, interp_ref.shape[1]
    pairs = (
        (rows_hbm, rows_ref),
        (points_hbm, points_ref),
        (weights_hbm, halo_ref.at[pl.ds(half, points)]),
        (interp_hbm, interp_ref),
        (ids_hbm, ids_ref),
        (ci_hbm, ci_ref),
        (flags_hbm, flags_ref),
    )
    copies = [pltpu.make_async_copy(source, place, arrived.at[i]) for i, (source, place) in enumerate(pairs)]
    for copy in copies:
        copy.start()
    leaf = lax.axis_index("leaf")
    core = leaf % 2
    cluster_count, picked = ids_ref.shape
    members = lax.axis_size("leaf") // cluster_count
    source_scale = -0.5 * scale_of(features)

    def packed(turned):
        n = turned.shape[1]
        return jnp.concatenate([turned[:, : n // 2], turned[:, n // 2 :]], axis=0).T

    def norms(turned):
        return source_scale * jnp.sum(turned * turned, axis=0, keepdims=True)

    for copy in copies:
        copy.wait()
    one = (
        lax.broadcasted_iota(jnp.int32, (points, skeletons), 0) == rows_ref[...]
    ).astype(F32).astype(BF16)
    skeleton = dot_nn(points_ref[...], one)
    weights_turned = halo_ref[half : half + points, :].astype(F32).T.astype(BF16)
    charges_turned = dot_nn(weights_turned, interp_ref[...]).astype(BF16)
    ids = ids_ref[pl.ds(leaf // members, 1), :] - (leaf % members) * skeletons
    chosen = (
        lax.broadcasted_iota(jnp.int32, (skeletons, picked), 0) == ids
    ).astype(F32).astype(BF16)
    cluster = dot_nn(skeleton.astype(BF16), chosen)
    sums = dot_nn(charges_turned, ci_ref[...]).T
    part = picked // 2
    rows = sum_ref.shape[0]
    for h in range(2):
        columns = slice(h * part, (h + 1) * part)
        place = slice(h * rows, h * rows + part)
        all_ref[place, :] = sums[columns]
        place = slice(h * rows + part, h * rows + part + part // 2)
        all_ref[place, :] = packed(cluster[:, columns])
        place = slice(h * rows + part + part // 2, (h + 1) * rows)
        all_ref[place, :] = norm_block(norms(cluster[:, columns]))
    sum_ref[...] = all_ref[pl.ds(core * rows, rows), :]
    send_ref[...] = all_ref[pl.ds((1 - core) * rows, rows), :].astype(BF16)
    sk_half, sk_norms = skeletons // 2, norm_rows(skeletons)
    sv_ref[:sk_half, :] = packed(skeleton).astype(BF16)
    block = norm_block(norms(skeleton))
    row = lax.broadcasted_iota(jnp.int32, block.shape, 0)
    block = jnp.where(row == sk_norms - 1, flag_row(flags_ref), block)
    sv_ref[sk_half : sk_half + sk_norms, :] = block.astype(BF16)
    sv_ref[sk_half + sk_norms :, :] = charges_turned.astype(F32).T.astype(BF16)
    wide = points_ref[...].astype(F32)
    halo_ref[:half, :] = packed(wide).astype(BF16)
    halo_ref[half + points :, :] = norm_block(norms(wide)).astype(BF16)


def add_kernel(with_skeleton, last, sum_ref, got_ref, *refs):
    rows = sum_ref.shape[0]
    total = sum_ref[...] + got_ref[:rows, :].astype(F32)
    if with_skeleton:
        own_ref, other_ref, *refs = refs
        send_ref = refs[0]
        points = (send_ref.shape[0] - rows) // 2
        send_ref[rows : rows + points, :] = own_ref[:points, :]
        send_ref[rows + points :, :] = other_ref[:points, :]
    refs[0][:rows, :] = total.astype(BF16)
    if not last:
        refs[1][...] = total


def near_kernel(stage, across, features, *refs):
    leaf = lax.axis_index("leaf")
    core, chip = leaf % 2, (leaf // 2) % 2
    side, beside = 1 - 2 * core, 1 - 2 * chip
    first = stage == 0 and not across
    if first:
        flags_ref, halo_ref, low_ref, high_ref, parts_ref, near_ref, mass_ref = refs
        half = near_ref.shape[0] // 2
        forms = target_forms(halo_ref[:half, :], features)
        for ref, form in zip((low_ref, high_ref, parts_ref), forms):
            ref[...] = form
        distance = 0
    else:
        before_ref, flags_ref, halo_ref, low_ref, high_ref, parts_ref, near_ref, mass_ref = refs
        half = near_ref.shape[0] // 2
        if across:
            distance = side if stage == 0 else -side
        else:
            distance = 2 * beside if stage == 1 else -2 * beside

    def tile():
        flag = flag_of(flags_ref, distance)
        norms = source_norms(halo_ref[3 * half :, :], 2 * half)
        mass_ref[...] = (halo_ref[half : 3 * half, :].astype(F32) * flag).astype(BF16)
        step = min(SOURCE_ROWS, half)
        for start in range(0, 2 * half, TARGET_ROWS):
            rows = slice(start, min(start + TARGET_ROWS, 2 * half))
            total = None
            for place in range(0, half, step):
                sources = ones_beside(halo_ref[place : place + step, :])
                for h, ref in enumerate((low_ref, high_ref)):
                    terms = norms[h][:, place : place + step]
                    values = kernel_values(ref[rows, :], parts_ref[rows, :], sources, terms, features)
                    term = dot_nn(values, mass_ref[h * half + place : h * half + place + step, :])
                    total = term if total is None else total + term
            near_ref[rows, :] = total if first else before_ref[rows, :] + total

    if across and stage > 0:
        pl.when(core != chip if stage == 1 else core == chip)(tile)
    else:
        tile()


def grouped(count, rows):
    step = max(1, SOURCE_ROWS // rows)
    return [range(i, min(i + step, count)) for i in range(0, count, step)]


def sibling_kernel(masks, reduced, features, skeletons, reach, partner_ref, core_ref, *refs):
    pieces, (own_ref, other_ref, send_ref, *form_refs) = refs[: len(masks)], refs[len(masks) :]
    leaf = lax.axis_index("leaf")
    half, points = skeletons // 2, skeletons // 2 + norm_rows(skeletons)
    start = partner_ref.shape[0] - 2 * points
    blocks = [
        (0, pieces[0][:points, :]),
        (reduced, partner_ref[start : start + points, :]),
        (1, core_ref[:points, :]),
        (reduced | 1, partner_ref[start + points :, :]),
    ]
    forms = zip(*[target_forms(block[:half], features) for _, block in blocks])
    low, high, parts = [jnp.concatenate(form, axis=0) for form in forms]
    for ref, form in zip(form_refs, (low, high, parts)):
        ref[...] = form[:skeletons]
    lane = lax.broadcasted_iota(jnp.int32, (1, LANES), 1)
    fields = [None] * len(blocks)
    for group in grouped(len(masks), half):
        sources = ones_beside(jnp.concatenate([pieces[i][:half, :] for i in group], axis=0))
        norms = [source_norms(pieces[i][half:points, :], skeletons) for i in group]
        mass = [pieces[i][points:, :].astype(F32) for i in group]
        masses = []
        for target, block in blocks:
            flags = block[points - 16 :].astype(F32)[15:16]
            kept = []
            for i in group:
                distance = (leaf ^ masks[i]) - (leaf ^ target)
                kept.append(1.0 - jnp.sum(jnp.where(lane == distance + reach, flags, 0.0), axis=1, keepdims=True))
            masses.append([(m * k).astype(BF16) for m, k in zip(mass, kept)])
        for h, targets in enumerate((low, high)):
            terms = jnp.concatenate([n[h] for n in norms], axis=1)
            values = kernel_values(targets, parts, sources, terms, features)
            for k in range(len(blocks)):
                both = jnp.concatenate([m[h * half : (h + 1) * half] for m in masses[k]], axis=0)
                term = dot_nn(values[k * skeletons : (k + 1) * skeletons], both)
                fields[k] = term if fields[k] is None else fields[k] + term
    own_ref[...] = fields[0]
    other_ref[...] = fields[1]
    send_ref[:skeletons, :] = fields[2].astype(BF16)
    send_ref[skeletons:, :] = fields[3].astype(BF16)


def field_kernel(own_ref, other_ref, got_ref, field_ref, send_ref):
    rows = own_ref.shape[0]
    field_ref[...] = own_ref[...] + got_ref[:rows, :].astype(F32)
    send_ref[...] = (other_ref[...] + got_ref[rows:, :].astype(F32)).astype(BF16)


def final_kernel(count, features, near_ref, interp_ref, low_ref, high_ref, parts_ref, own_ref, got_ref, *refs):
    packs, out_ref = refs[:count], refs[count]
    low, high, parts = low_ref[...], high_ref[...], parts_ref[...]
    half = max(r for r in range(1, packs[0].shape[0]) if 3 * r + norm_rows(2 * r) <= packs[0].shape[0])
    field = own_ref[...] + got_ref[...].astype(F32)
    for group in grouped(count, half):
        sources = ones_beside(jnp.concatenate([packs[i][2 * half : 3 * half, :] for i in group], axis=0))
        norms = [source_norms(packs[i][3 * half :, :], 2 * half) for i in group]
        for h, targets in enumerate((low, high)):
            terms = jnp.concatenate([n[h] for n in norms], axis=1)
            values = kernel_values(targets, parts, sources, terms, features)
            mass = jnp.concatenate([packs[i][h * half : (h + 1) * half, :] for i in group], axis=0)
            field += dot_nn(values, mass)
    coarse = field.astype(BF16)
    out_ref[...] = (near_ref[...] + dot_nn(interp_ref[...], coarse)).astype(out_ref.dtype)


def on_device(points, weights, interp, cluster_interp, skeleton_rows, near_flags, cluster_rows):
    leaves, groups = lax.axis_size("leaf"), lax.axis_size("group")
    leaf_points, features = points.shape
    columns = weights.shape[1]
    skeletons = interp.shape[1]
    cluster_count, picked = cluster_rows.shape
    members = leaves // cluster_count
    core_mask, chip_mask, reduced = 1, 2, 4
    half, part = leaf_points // 2, picked // 2
    sum_rows = part + part // 2 + norm_rows(part)
    sv_points = skeletons // 2 + norm_rows(skeletons)

    arguments = [points.T, weights, interp, cluster_interp, skeleton_rows, near_flags, cluster_rows]
    outs = [
        ((half + leaf_points + norm_rows(leaf_points), columns), BF16),
        ((sv_points + skeletons, columns), BF16),
        ((sum_rows, columns), F32),
        ((sum_rows, columns), BF16),
        (near_flags.shape, near_flags.dtype),
    ]
    scratch = [(x.shape, x.dtype) for x in (arguments[0], interp, cluster_interp, skeleton_rows, cluster_rows)]
    scratch += [((2 * sum_rows, columns), F32)]
    halo, skeleton, cluster_sum, cluster_send, flags = pl.pallas_call(
        prepare_kernel,
        out_shape=[jax.ShapeDtypeStruct(shape, dtype) for shape, dtype in outs],
        in_specs=[pl.BlockSpec(memory_space=pltpu.HBM) for _ in arguments],
        out_specs=[vmem() for _ in outs],
        scratch_shapes=[pltpu.VMEM(shape, dtype) for shape, dtype in scratch]
        + [pltpu.SemaphoreType.DMA((len(arguments),))],
        compiler_params=pltpu.CompilerParams(vmem_limit_bytes=VMEM_BYTES),
        cost_estimate=pl.CostEstimate(flops=10**6, bytes_accessed=0, transcendentals=0),
    )(*[pltpu.with_memory_space_constraint(x, pltpu.HBM) for x in arguments])

    have, done = {}, {}
    add_masks = [1 << i for i in reversed(range(1, members.bit_length() - 1))]
    adds = dict(zip(("first_add", "add_a", "add_b", "add_c"), add_masks + [0]))
    gather_masks = [1 << i for i in reversed(range(2, leaves.bit_length() - 1)) if 1 << i != reduced]
    piece_masks = [m for m in range(leaves) if not m & (reduced | core_mask)]
    reach = (near_flags.shape[1] - 1) // 2
    ahead = [(i, i + 4) for i in range(leaves - 4) if i & chip_mask == 0]
    behind = [(i, i - 4) for i in range(4, leaves) if i & chip_mask != 0]
    tile = ((leaf_points, columns), BF16)
    near_ins = {
        "near_core": (0, True, "halo_core"),
        "near_beside": (1, False, "halo_next"),
        "near_across": (1, True, "halo_across"),
        "near_far": (2, False, "halo_far"),
        "near_last": (2, True, "halo_last"),
    }

    def get(name):
        if name not in have:
            value = arrive(name)
            if name in RELEASES:
                value = hand_on(value, *[done[x] if x in done else get(x) for x in RELEASES[name]])
            have[name] = value
        return have[name]

    def arrive(name):
        if name == "sv_1":
            return xor_exchange(skeleton, "leaf", core_mask)
        if name.startswith("sv_"):
            mask = int(name[3:])
            if mask == 0:
                return skeleton
            step = core_mask if mask & core_mask else chip_mask if mask & chip_mask else mask & -mask
            return xor_exchange(get(f"sv_{mask ^ step}"), "leaf", step)
        if name == "halo_core":
            return xor_exchange(halo, "leaf", core_mask)
        if name == "halo_beside":
            return xor_exchange(halo, "leaf", chip_mask)
        if name == "halo_next":
            return get("halo_beside")
        if name == "halo_across":
            return xor_exchange(get("halo_next"), "leaf", core_mask)
        if name == "halo_far":
            return lax.ppermute(get("halo_next"), "leaf", ahead + behind)
        if name == "halo_last":
            return xor_exchange(get("halo_far"), "leaf", core_mask)
        if name == "field":
            return xor_exchange(have["field_send"], "leaf", reduced)
        if name.startswith("sum_"):
            return xor_exchange(have["sum_send"], "leaf", int(name[4:]))
        if name == "packs":
            own_group = [have["sum_send"]]
            mask = members
            while mask < leaves:
                own_group += [xor_exchange(pack, "leaf", mask) for pack in own_group]
                mask *= 2
            packs = []
            for shift in range(1, groups):
                order = [(i, (i + shift) % groups) for i in range(groups)]
                packs += [lax.ppermute(pack, "group", order) for pack in own_group]
            return jnp.concatenate(packs, axis=0) if len(packs) > 1 else packs[0]
        if name == "packs_core":
            return xor_exchange(get("packs"), "leaf", core_mask)
        raise KeyError(name)

    have["sum"], have["sum_send"] = cluster_sum, cluster_send
    have["sum_1"] = xor_exchange(cluster_send, "leaf", core_mask)
    received, token = "sum_1", None
    for name, work in ORDER.items():
        after = ([token] if token is not None else []) + [get(x) for x in DEADLINES.get(name, ())]
        if name in adds:
            mask, last = adds[name], adds[name] == 0
            with_skeleton = mask == reduced
            rows = sum_rows + (2 * sv_points if with_skeleton else 0)
            outs = [((rows, columns), BF16)] + ([] if last else [((sum_rows, columns), F32)])
            ins = [have["sum"], have[received]] + ([get("sv_0"), get("sv_1")] if with_skeleton else [])
            body = functools.partial(add_kernel, with_skeleton, last)
            have["sum_send"], *total = call(body, outs, ins, after=after, work=work)
            token = have["sum_send"]
            if not last:
                have["sum"], received = total[0], f"sum_{mask}"
                have[received] = arrive(received)
            else:
                get("packs")
        elif name == "near_self":
            *targets, near = call(
                functools.partial(near_kernel, 0, False, features),
                [tile, tile, tile, ((leaf_points, columns), F32)],
                [flags, halo],
                scratch=[((leaf_points, columns), BF16)],
                after=after,
                work=work,
            )
            token = near
        elif name in near_ins:
            stage, across, source = near_ins[name]
            (near,) = call(
                functools.partial(near_kernel, stage, across, features),
                [((leaf_points, columns), F32)],
                [near, flags, get(source), *targets],
                scratch=[((leaf_points, columns), BF16)],
                after=after if token is not near else after[1:],
                in_place=True,
                work=work,
            )
            token = near
        elif name == "sibling":
            *fields, have["field_send"], low, high, parts = call(
                functools.partial(sibling_kernel, piece_masks, reduced, features, skeletons, reach),
                [((skeletons, columns), F32)] * 2
                + [((2 * skeletons, columns), BF16)]
                + [((skeletons, columns), BF16)] * 3,
                [have[f"sum_{reduced}"], get("sv_1")] + [get(f"sv_{m}") for m in piece_masks],
                after=after,
                work=work,
            )
            token = fields[0]
            have["field_core"] = xor_exchange(have["field_send"], "leaf", core_mask)
        elif name == "field":
            field, have["field_send"] = call(
                field_kernel,
                [((skeletons, columns), F32), ((skeletons, columns), BF16)],
                fields + [have["field_core"]],
                after=after,
                work=work,
            )
            token = field
            get("field")
        elif name == "final":
            packs = [get("packs"), get("packs_core")]
            packs = [p[i : i + sum_rows] for p in packs for i in range(0, p.shape[0], sum_rows)]
            (token,) = call(
                functools.partial(final_kernel, len(packs), features),
                [((leaf_points, columns), BF16)],
                [near, interp, low, high, parts, field, get("field")] + packs,
                work=work,
            )
        done[name] = token
    return token


def solution(mesh):
    placed = (P(("group", "leaf"), None),) * 6 + (P("group", None),)
    return jax.shard_map(
        on_device, mesh=mesh, in_specs=placed, out_specs=P(("group", "leaf"), None), check_vma=False
    )
```

```python
import functools
import math

import jax
import jax.numpy as jnp
from jax import lax
from jax.experimental import pallas as pl
from jax.experimental.pallas import tpu as pltpu
from jax.sharding import PartitionSpec as P

BF16 = jnp.bfloat16
F32 = jnp.float32
VMEM_BYTES = 24 * 1024 * 1024
LANES = 128
TARGET_ROWS = 512
SOURCE_ROWS = 512
ORDER = {
    "first_add": 8000000000,
    "near_self": 2000000000,
    "near_core": 2000000000,
    "near_beside": 4000000000,
    "add_a": 1000000,
    "add_b": 1000000,
    "sibling": 2000000000,
    "near_across": 2000000000,
    "add_c": 10000000,
    "field": 1000000,
    "near_far": 2000000000,
    "near_last": 2000000000,
    "final": 2000000000,
}
DEADLINES = {
    "sibling": ["sv_10"],
    "add_c": ["sv_8"],
}
RELEASES = {"sv_0": ["first_add"], "halo_next": ["near_core"], "halo_far": ["field", "packs"]}


def vmem():
    return pl.BlockSpec(memory_space=pltpu.VMEM)


def call(body, outs, ins, scratch=(), after=(), in_place=False, work=10**6):
    waits = len(after)
    return pl.pallas_call(
        lambda *refs: body(*refs[waits:]),
        out_shape=[jax.ShapeDtypeStruct(shape, dtype) for shape, dtype in outs],
        in_specs=[pl.BlockSpec(memory_space=pl.ANY) for _ in after] + [vmem() for _ in ins],
        out_specs=[vmem() for _ in outs],
        scratch_shapes=[pltpu.VMEM(shape, dtype) for shape, dtype in scratch],
        input_output_aliases={waits: 0} if in_place else {},
        compiler_params=pltpu.CompilerParams(vmem_limit_bytes=VMEM_BYTES),
        cost_estimate=pl.CostEstimate(flops=work, bytes_accessed=0, transcendentals=0),
    )(*after, *ins)


def hand_on(value, *after):
    return pl.pallas_call(
        lambda *refs: None,
        out_shape=jax.ShapeDtypeStruct(value.shape, value.dtype),
        in_specs=[vmem()] + [pl.BlockSpec(memory_space=pl.ANY) for _ in after],
        out_specs=vmem(),
        input_output_aliases={0: 0},
        compiler_params=pltpu.CompilerParams(vmem_limit_bytes=VMEM_BYTES),
        cost_estimate=pl.CostEstimate(flops=0, bytes_accessed=0, transcendentals=0),
    )(value, *after)


def dot_nt(a, b):
    return lax.dot_general(a, b, (((1,), (1,)), ((), ())), preferred_element_type=F32)


def dot_nn(a, b):
    return jnp.dot(a, b, preferred_element_type=F32)


def xor_exchange(value, axis, mask):
    return lax.ppermute(value, axis, [(i, i ^ mask) for i in range(lax.axis_size(axis))])


def up16(rows):
    return -(-rows // 16) * 16


def norm_rows(points):
    return up16(3 * points // LANES)


def scale_of(features):
    return 4.0 / features * math.log2(math.e)


def three_parts(values):
    high = values.astype(BF16).astype(F32)
    rest = values - high
    middle = rest.astype(BF16).astype(F32)
    return high, middle, rest - middle


def norm_block(norms):
    count = norms.shape[1] // LANES
    parts = [
        part[:, i * LANES : (i + 1) * LANES] for part in three_parts(norms) for i in range(count)
    ]
    rest = norm_rows(norms.shape[1]) - len(parts)
    return jnp.concatenate(parts + [jnp.zeros((rest, LANES), F32)], axis=0)


def source_norms(block, points):
    count = points // LANES
    block = block.astype(F32)
    rows = block[:count] + block[count : 2 * count] + block[2 * count : 3 * count]
    return tuple(
        jnp.concatenate([rows[i : i + 1] for i in range(h * count // 2, (h + 1) * count // 2)], axis=1)
        for h in range(2)
    )


def target_forms(packed, features):
    wide = packed.astype(F32)
    turned = pltpu.roll(wide, features, 1)
    lane = lax.broadcasted_iota(jnp.int32, wide.shape, 1)
    low, high, norms = [], [], []
    for first, second in ((wide, turned), (turned, wide)):
        kept = jnp.where(lane < features, first, 0.0)
        low.append(kept)
        high.append(jnp.where(lane >= features, second, 0.0))
        parts = three_parts(-0.5 * jnp.sum(kept * kept, axis=1, keepdims=True))
        norms.append(
            jnp.where(lane == 0, parts[0], jnp.where(lane == 1, parts[1], jnp.where(lane == 2, parts[2], 0.0)))
        )
    return tuple(jnp.concatenate(form, axis=0).astype(BF16) for form in (low, high, norms))


def ones_beside(packed):
    lane = lax.broadcasted_iota(jnp.int32, packed.shape, 1)
    return jnp.concatenate([packed, jnp.where(lane < 3, 1.0, 0.0).astype(BF16)], axis=1)


def kernel_values(targets, parts, sources, norms, features):
    exponent = dot_nt(jnp.concatenate([targets, parts], axis=1), sources) * scale_of(features) + norms
    return jnp.exp2(exponent).astype(BF16)


def flag_of(flags_ref, distance):
    columns = flags_ref.shape[1]
    lane = lax.broadcasted_iota(jnp.int32, (1, columns), 1)
    here = lane == distance + (columns - 1) // 2
    return jnp.sum(jnp.where(here, flags_ref[...], 0).astype(F32), axis=1, keepdims=True)


def flag_row(flags_ref):
    columns = flags_ref.shape[1]
    lane = lax.broadcasted_iota(jnp.int32, (1, LANES), 1)
    row = jnp.zeros((1, LANES), F32)
    for column in range(columns):
        row = jnp.where(lane == column, flag_of(flags_ref, column - (columns - 1) // 2), row)
    return row


def prepare_kernel(
    points_hbm, weights_hbm, interp_hbm, ci_hbm, rows_hbm, flags_hbm, ids_hbm,
    halo_ref, sv_ref, sum_ref, send_ref, flags_ref,
    points_ref, interp_ref, ci_ref, rows_ref, ids_ref, all_ref, arrived,
):
    features, points = points_ref.shape
    half, skeletons = points // 2, interp_ref.shape[1]
    pairs = (
        (rows_hbm, rows_ref),
        (points_hbm, points_ref),
        (weights_hbm, halo_ref.at[pl.ds(half, points)]),
        (interp_hbm, interp_ref),
        (ids_hbm, ids_ref),
        (ci_hbm, ci_ref),
        (flags_hbm, flags_ref),
    )
    copies = [pltpu.make_async_copy(source, place, arrived.at[i]) for i, (source, place) in enumerate(pairs)]
    for copy in copies:
        copy.start()
    leaf = lax.axis_index("leaf")
    core = leaf % 2
    cluster_count, picked = ids_ref.shape
    members = lax.axis_size("leaf") // cluster_count
    source_scale = -0.5 * scale_of(features)

    def packed(turned):
        n = turned.shape[1]
        return jnp.concatenate([turned[:, : n // 2], turned[:, n // 2 :]], axis=0).T

    def norms(turned):
        return source_scale * jnp.sum(turned * turned, axis=0, keepdims=True)

    for copy in copies:
        copy.wait()
    one = (
        lax.broadcasted_iota(jnp.int32, (points, skeletons), 0) == rows_ref[...]
    ).astype(F32).astype(BF16)
    skeleton = dot_nn(points_ref[...], one)
    weights_turned = halo_ref[half : half + points, :].astype(F32).T.astype(BF16)
    charges_turned = dot_nn(weights_turned, interp_ref[...]).astype(BF16)
    ids = ids_ref[pl.ds(leaf // members, 1), :] - (leaf % members) * skeletons
    chosen = (
        lax.broadcasted_iota(jnp.int32, (skeletons, picked), 0) == ids
    ).astype(F32).astype(BF16)
    cluster = dot_nn(skeleton.astype(BF16), chosen)
    sums = dot_nn(charges_turned, ci_ref[...]).T
    part = picked // 2
    rows = sum_ref.shape[0]
    for h in range(2):
        columns = slice(h * part, (h + 1) * part)
        place = slice(h * rows, h * rows + part)
        all_ref[place, :] = sums[columns]
        place = slice(h * rows + part, h * rows + part + part // 2)
        all_ref[place, :] = packed(cluster[:, columns])
        place = slice(h * rows + part + part // 2, (h + 1) * rows)
        all_ref[place, :] = norm_block(norms(cluster[:, columns]))
    sum_ref[...] = all_ref[pl.ds(core * rows, rows), :]
    send_ref[...] = all_ref[pl.ds((1 - core) * rows, rows), :].astype(BF16)
    sk_half, sk_norms = skeletons // 2, norm_rows(skeletons)
    sv_ref[:sk_half, :] = packed(skeleton).astype(BF16)
    block = norm_block(norms(skeleton))
    row = lax.broadcasted_iota(jnp.int32, block.shape, 0)
    block = jnp.where(row == sk_norms - 1, flag_row(flags_ref), block)
    sv_ref[sk_half : sk_half + sk_norms, :] = block.astype(BF16)
    sv_ref[sk_half + sk_norms :, :] = charges_turned.astype(F32).T.astype(BF16)
    wide = points_ref[...].astype(F32)
    halo_ref[:half, :] = packed(wide).astype(BF16)
    halo_ref[half + points :, :] = norm_block(norms(wide)).astype(BF16)


def add_kernel(with_skeleton, last, sum_ref, got_ref, *refs):
    rows = sum_ref.shape[0]
    total = sum_ref[...] + got_ref[:rows, :].astype(F32)
    if with_skeleton:
        own_ref, other_ref, *refs = refs
        send_ref = refs[0]
        points = (send_ref.shape[0] - rows) // 2
        send_ref[rows : rows + points, :] = own_ref[:points, :]
        send_ref[rows + points :, :] = other_ref[:points, :]
    refs[0][:rows, :] = total.astype(BF16)
    if not last:
        refs[1][...] = total


def near_kernel(stage, across, features, *refs):
    leaf = lax.axis_index("leaf")
    core, chip = leaf % 2, (leaf // 2) % 2
    side, beside = 1 - 2 * core, 1 - 2 * chip
    first = stage == 0 and not across
    if first:
        flags_ref, halo_ref, low_ref, high_ref, parts_ref, near_ref, mass_ref = refs
        half = near_ref.shape[0] // 2
        forms = target_forms(halo_ref[:half, :], features)
        for ref, form in zip((low_ref, high_ref, parts_ref), forms):
            ref[...] = form
        distance = 0
    else:
        before_ref, flags_ref, halo_ref, low_ref, high_ref, parts_ref, near_ref, mass_ref = refs
        half = near_ref.shape[0] // 2
        if across:
            distance = side if stage == 0 else -side
        else:
            distance = 2 * beside if stage == 1 else -2 * beside

    def tile():
        flag = flag_of(flags_ref, distance)
        norms = source_norms(halo_ref[3 * half :, :], 2 * half)
        mass_ref[...] = (halo_ref[half : 3 * half, :].astype(F32) * flag).astype(BF16)
        step = min(SOURCE_ROWS, half)
        for start in range(0, 2 * half, TARGET_ROWS):
            rows = slice(start, min(start + TARGET_ROWS, 2 * half))
            total = None
            for place in range(0, half, step):
                sources = ones_beside(halo_ref[place : place + step, :])
                for h, ref in enumerate((low_ref, high_ref)):
                    terms = norms[h][:, place : place + step]
                    values = kernel_values(ref[rows, :], parts_ref[rows, :], sources, terms, features)
                    term = dot_nn(values, mass_ref[h * half + place : h * half + place + step, :])
                    total = term if total is None else total + term
            near_ref[rows, :] = total if first else before_ref[rows, :] + total

    if across and stage > 0:
        pl.when(core != chip if stage == 1 else core == chip)(tile)
    else:
        tile()


def grouped(count, rows):
    step = max(1, SOURCE_ROWS // rows)
    return [range(i, min(i + step, count)) for i in range(0, count, step)]


def sibling_kernel(masks, reduced, features, skeletons, reach, partner_ref, core_ref, *refs):
    pieces, (own_ref, other_ref, send_ref, *form_refs) = refs[: len(masks)], refs[len(masks) :]
    leaf = lax.axis_index("leaf")
    half, points = skeletons // 2, skeletons // 2 + norm_rows(skeletons)
    start = partner_ref.shape[0] - 2 * points
    blocks = [
        (0, pieces[0][:points, :]),
        (reduced, partner_ref[start : start + points, :]),
        (1, core_ref[:points, :]),
        (reduced | 1, partner_ref[start + points :, :]),
    ]
    forms = zip(*[target_forms(block[:half], features) for _, block in blocks])
    low, high, parts = [jnp.concatenate(form, axis=0) for form in forms]
    for ref, form in zip(form_refs, (low, high, parts)):
        ref[...] = form[:skeletons]
    lane = lax.broadcasted_iota(jnp.int32, (1, LANES), 1)
    fields = [None] * len(blocks)
    for group in grouped(len(masks), half):
        sources = ones_beside(jnp.concatenate([pieces[i][:half, :] for i in group], axis=0))
        norms = [source_norms(pieces[i][half:points, :], skeletons) for i in group]
        mass = [pieces[i][points:, :].astype(F32) for i in group]
        masses = []
        for target, block in blocks:
            flags = block[points - 16 :].astype(F32)[15:16]
            kept = []
            for i in group:
                distance = (leaf ^ masks[i]) - (leaf ^ target)
                kept.append(1.0 - jnp.sum(jnp.where(lane == distance + reach, flags, 0.0), axis=1, keepdims=True))
            masses.append([(m * k).astype(BF16) for m, k in zip(mass, kept)])
        for h, targets in enumerate((low, high)):
            terms = jnp.concatenate([n[h] for n in norms], axis=1)
            values = kernel_values(targets, parts, sources, terms, features)
            for k in range(len(blocks)):
                both = jnp.concatenate([m[h * half : (h + 1) * half] for m in masses[k]], axis=0)
                term = dot_nn(values[k * skeletons : (k + 1) * skeletons], both)
                fields[k] = term if fields[k] is None else fields[k] + term
    own_ref[...] = fields[0]
    other_ref[...] = fields[1]
    send_ref[:skeletons, :] = fields[2].astype(BF16)
    send_ref[skeletons:, :] = fields[3].astype(BF16)


def field_kernel(own_ref, other_ref, got_ref, field_ref, send_ref):
    rows = own_ref.shape[0]
    field_ref[...] = own_ref[...] + got_ref[:rows, :].astype(F32)
    send_ref[...] = (other_ref[...] + got_ref[rows:, :].astype(F32)).astype(BF16)


def final_kernel(count, features, near_ref, interp_ref, low_ref, high_ref, parts_ref, own_ref, got_ref, *refs):
    packs, out_ref = refs[:count], refs[count]
    low, high, parts = low_ref[...], high_ref[...], parts_ref[...]
    half = max(r for r in range(1, packs[0].shape[0]) if 3 * r + norm_rows(2 * r) <= packs[0].shape[0])
    field = own_ref[...] + got_ref[...].astype(F32)
    for group in grouped(count, half):
        sources = ones_beside(jnp.concatenate([packs[i][2 * half : 3 * half, :] for i in group], axis=0))
        norms = [source_norms(packs[i][3 * half :, :], 2 * half) for i in group]
        for h, targets in enumerate((low, high)):
            terms = jnp.concatenate([n[h] for n in norms], axis=1)
            values = kernel_values(targets, parts, sources, terms, features)
            mass = jnp.concatenate([packs[i][h * half : (h + 1) * half, :] for i in group], axis=0)
            field += dot_nn(values, mass)
    coarse = field.astype(BF16)
    out_ref[...] = (near_ref[...] + dot_nn(interp_ref[...], coarse)).astype(out_ref.dtype)


def on_device(points, weights, interp, cluster_interp, skeleton_rows, near_flags, cluster_rows):
    leaves, groups = lax.axis_size("leaf"), lax.axis_size("group")
    leaf_points, features = points.shape
    columns = weights.shape[1]
    skeletons = interp.shape[1]
    cluster_count, picked = cluster_rows.shape
    members = leaves // cluster_count
    core_mask, chip_mask, reduced = 1, 2, 4
    half, part = leaf_points // 2, picked // 2
    sum_rows = part + part // 2 + norm_rows(part)
    sv_points = skeletons // 2 + norm_rows(skeletons)

    arguments = [points.T, weights, interp, cluster_interp, skeleton_rows, near_flags, cluster_rows]
    outs = [
        ((half + leaf_points + norm_rows(leaf_points), columns), BF16),
        ((sv_points + skeletons, columns), BF16),
        ((sum_rows, columns), F32),
        ((sum_rows, columns), BF16),
        (near_flags.shape, near_flags.dtype),
    ]
    scratch = [(x.shape, x.dtype) for x in (arguments[0], interp, cluster_interp, skeleton_rows, cluster_rows)]
    scratch += [((2 * sum_rows, columns), F32)]
    halo, skeleton, cluster_sum, cluster_send, flags = pl.pallas_call(
        prepare_kernel,
        out_shape=[jax.ShapeDtypeStruct(shape, dtype) for shape, dtype in outs],
        in_specs=[pl.BlockSpec(memory_space=pltpu.HBM) for _ in arguments],
        out_specs=[vmem() for _ in outs],
        scratch_shapes=[pltpu.VMEM(shape, dtype) for shape, dtype in scratch]
        + [pltpu.SemaphoreType.DMA((len(arguments),))],
        compiler_params=pltpu.CompilerParams(vmem_limit_bytes=VMEM_BYTES),
        cost_estimate=pl.CostEstimate(flops=10**6, bytes_accessed=0, transcendentals=0),
    )(*[pltpu.with_memory_space_constraint(x, pltpu.HBM) for x in arguments])

    have, done = {}, {}
    add_masks = [1 << i for i in reversed(range(1, members.bit_length() - 1))]
    adds = dict(zip(("first_add", "add_a", "add_b", "add_c"), add_masks + [0]))
    gather_masks = [1 << i for i in reversed(range(2, leaves.bit_length() - 1)) if 1 << i != reduced]
    piece_masks = [m for m in range(leaves) if not m & (reduced | core_mask)]
    reach = (near_flags.shape[1] - 1) // 2
    ahead = [(i, i + 4) for i in range(leaves - 4) if i & chip_mask == 0]
    behind = [(i, i - 4) for i in range(4, leaves) if i & chip_mask != 0]
    tile = ((leaf_points, columns), BF16)
    near_ins = {
        "near_core": (0, True, "halo_core"),
        "near_beside": (1, False, "halo_next"),
        "near_across": (1, True, "halo_across"),
        "near_far": (2, False, "halo_far"),
        "near_last": (2, True, "halo_last"),
    }

    def get(name):
        if name not in have:
            value = arrive(name)
            if name in RELEASES:
                value = hand_on(value, *[done[x] if x in done else get(x) for x in RELEASES[name]])
            have[name] = value
        return have[name]

    def arrive(name):
        if name == "sv_1":
            return xor_exchange(skeleton, "leaf", core_mask)
        if name.startswith("sv_"):
            mask = int(name[3:])
            if mask == 0:
                return skeleton
            step = core_mask if mask & core_mask else chip_mask if mask & chip_mask else mask & -mask
            return xor_exchange(get(f"sv_{mask ^ step}"), "leaf", step)
        if name == "halo_core":
            return xor_exchange(halo, "leaf", core_mask)
        if name == "halo_beside":
            return xor_exchange(halo, "leaf", chip_mask)
        if name == "halo_next":
            return get("halo_beside")
        if name == "halo_across":
            return xor_exchange(get("halo_next"), "leaf", core_mask)
        if name == "halo_far":
            return lax.ppermute(get("halo_next"), "leaf", ahead + behind)
        if name == "halo_last":
            return xor_exchange(get("halo_far"), "leaf", core_mask)
        if name == "field":
            return xor_exchange(have["field_send"], "leaf", reduced)
        if name.startswith("sum_"):
            return xor_exchange(have["sum_send"], "leaf", int(name[4:]))
        if name == "packs":
            own_group = [have["sum_send"]]
            mask = members
            while mask < leaves:
                own_group += [xor_exchange(pack, "leaf", mask) for pack in own_group]
                mask *= 2
            packs = []
            for shift in range(1, groups):
                order = [(i, (i + shift) % groups) for i in range(groups)]
                packs += [lax.ppermute(pack, "group", order) for pack in own_group]
            return jnp.concatenate(packs, axis=0) if len(packs) > 1 else packs[0]
        if name == "packs_core":
            return xor_exchange(get("packs"), "leaf", core_mask)
        raise KeyError(name)

    have["sum"], have["sum_send"] = cluster_sum, cluster_send
    have["sum_1"] = xor_exchange(cluster_send, "leaf", core_mask)
    received, token = "sum_1", None
    for name, work in ORDER.items():
        after = ([token] if token is not None else []) + [get(x) for x in DEADLINES.get(name, ())]
        if name in adds:
            mask, last = adds[name], adds[name] == 0
            with_skeleton = mask == reduced
            rows = sum_rows + (2 * sv_points if with_skeleton else 0)
            outs = [((rows, columns), BF16)] + ([] if last else [((sum_rows, columns), F32)])
            ins = [have["sum"], have[received]] + ([get("sv_0"), get("sv_1")] if with_skeleton else [])
            body = functools.partial(add_kernel, with_skeleton, last)
            have["sum_send"], *total = call(body, outs, ins, after=after, work=work)
            token = have["sum_send"]
            if not last:
                have["sum"], received = total[0], f"sum_{mask}"
                have[received] = arrive(received)
            else:
                get("packs")
        elif name == "near_self":
            *targets, near = call(
                functools.partial(near_kernel, 0, False, features),
                [tile, tile, tile, ((leaf_points, columns), F32)],
                [flags, halo],
                scratch=[((leaf_points, columns), BF16)],
                after=after,
                work=work,
            )
            token = near
        elif name in near_ins:
            stage, across, source = near_ins[name]
            (near,) = call(
                functools.partial(near_kernel, stage, across, features),
                [((leaf_points, columns), F32)],
                [near, flags, get(source), *targets],
                scratch=[((leaf_points, columns), BF16)],
                after=after if token is not near else after[1:],
                in_place=True,
                work=work,
            )
            token = near
        elif name == "sibling":
            *fields, have["field_send"], low, high, parts = call(
                functools.partial(sibling_kernel, piece_masks, reduced, features, skeletons, reach),
                [((skeletons, columns), F32)] * 2
                + [((2 * skeletons, columns), BF16)]
                + [((skeletons, columns), BF16)] * 3,
                [have[f"sum_{reduced}"], get("sv_1")] + [get(f"sv_{m}") for m in piece_masks],
                after=after,
                work=work,
            )
            token = fields[0]
            have["field_core"] = xor_exchange(have["field_send"], "leaf", core_mask)
        elif name == "field":
            field, have["field_send"] = call(
                field_kernel,
                [((skeletons, columns), F32), ((skeletons, columns), BF16)],
                fields + [have["field_core"]],
                after=after,
                work=work,
            )
            token = field
            get("field")
        elif name == "final":
            packs = [get("packs"), get("packs_core")]
            packs = [p[i : i + sum_rows] for p in packs for i in range(0, p.shape[0], sum_rows)]
            (token,) = call(
                functools.partial(final_kernel, len(packs), features),
                [((leaf_points, columns), BF16)],
                [near, interp, low, high, parts, field, get("field")] + packs,
                work=work,
            )
        done[name] = token
    return token


def solution(mesh):
    placed = (P(("group", "leaf"), None),) * 6 + (P("group", None),)
    return jax.shard_map(
        on_device, mesh=mesh, in_specs=placed, out_specs=P(("group", "leaf"), None), check_vma=False
    )
```
